32 devices in a mesh: wide: 16 (over z, y, core), narrow: 2 (over x).
Axes of the slice: x: 2, y: 2, z: 4, core: 2. Of those that a mesh axis runs over, the one named last changes fastest.
Arguments:
- inputs: bfloat16 [32, 1024, 1024], P(('wide', 'narrow')), may hold values from -6 to 6
- norm_first: bfloat16 [1024], P(('wide', 'narrow')), may hold values from 0.5 to 1.5
- w_query: bfloat16 [1024, 1024], P(('wide', 'narrow')), may hold values from -0.046875 to 0.046875
- w_key: bfloat16 [1024, 1024], P(('wide', 'narrow')), may hold values from -0.1875 to 0.1875
- w_value: bfloat16 [1024, 1024], P(('wide', 'narrow')), may hold values from -0.1875 to 0.1875
- w_out: bfloat16 [1024, 1024], P(('wide', 'narrow')), may hold values from -1 to 1
- rel_table: bfloat16 [512], P(('wide', 'narrow')), may hold values from -4 to 4
- x_table: bfloat16 [512], P(('wide', 'narrow')), may hold values from -4 to 4
- y_table: bfloat16 [512], P(('wide', 'narrow')), may hold values from -4 to 4
- norm_second: bfloat16 [1024], P(('wide', 'narrow')), may hold values from 0.5 to 1.5
- w_gate: bfloat16 [1024, 2816], P(('wide', 'narrow')), may hold values from -0.1875 to 0.1875
- w_up: bfloat16 [1024, 2816], P(('wide', 'narrow')), may hold values from -0.1875 to 0.1875
- w_down: bfloat16 [2816, 1024], P(('wide', 'narrow')), may hold values from -0.109375 to 0.109375
- lengths: int32 [32], P(('wide', 'narrow')), may hold values from 320 to 1024, as said below
- boxes: int32 [32, 2, 1024], P(('wide', 'narrow')), may hold values from 0 to 1000
- cotangent: bfloat16 [32, 1024, 1024], P(('wide', 'narrow')), may hold values from -6 to 6
Outputs:
- output: bfloat16 [32, 1024, 1024], P(('wide', 'narrow'))
- grad_inputs: float32 [32, 1024, 1024], P(('wide', 'narrow'))
- grad_norm_first: float32 [1024], P(('wide', 'narrow'))
- grad_w_query: float32 [1024, 1024], P(('wide', 'narrow'))
- grad_w_key: float32 [1024, 1024], P(('wide', 'narrow'))
- grad_w_value: float32 [1024, 1024], P(('wide', 'narrow'))
- grad_w_out: float32 [1024, 1024], P(('wide', 'narrow'))
- grad_rel_table: float32 [512], P(('wide', 'narrow'))
- grad_x_table: float32 [512], P(('wide', 'narrow'))
- grad_y_table: float32 [512], P(('wide', 'narrow'))
- grad_norm_second: float32 [1024], P(('wide', 'narrow'))
- grad_w_gate: float32 [1024, 2816], P(('wide', 'narrow'))
- grad_w_up: float32 [1024, 2816], P(('wide', 'narrow'))
- grad_w_down: float32 [2816, 1024], P(('wide', 'narrow'))
The draws below stay inside these ranges and needn't reach their ends.
Inputs may be any that keep to these rules, and one draw needn't show every extreme that they name: `lengths`: every sequence has 320 to 704 true tokens, except 32 // 7 sequences placed anywhere, which are full at 1024.
All inputs are finite; a program needn't handle non-finite values.
Results may differ from the reference program's by a relative error of at most 0.014.
The reference program's roundings to bfloat16 on the way count: a program that leaves them out, or rounds other values in their place, can miss the bound.
Values may be sent and summed in bfloat16 or wider, within the bound.
No kernel may reach another device: no remote copies, remote signals or barrier semaphores. Data moves between devices by JAX's collectives and lax.ppermute only.
A program may use at most 384 MiB of HBM per device.

```python
import jax
import jax.numpy as jnp
import numpy as np
from jax import lax

D = 1024
HEADS = 16
HEAD_DIM = 64
FF = 2816
BUCKETS = 32
SLOTS = 1024
INNER = 1024
SEQS = 32


def draw_lengths(key, part):
    key = jax.random.fold_in(key, 11)
    first, second = jax.random.split(key)
    base = jax.random.randint(first, (SEQS,), SLOTS * 5 // 16, SLOTS * 11 // 16 + 1)
    order = jax.random.permutation(second, SEQS)
    full = order < SEQS // 7
    return jnp.where(full, SLOTS, base).astype(jnp.int32)


def touch_ends(drawn, key, low, largest):
    longest = drawn.shape.index(max(drawn.shape))
    spots = []
    for shift in (0, 1):
        where = [jax.random.randint(jax.random.fold_in(key, axis), (), 0, length) for axis, length in enumerate(drawn.shape)]
        where[longest] = (where[longest] + shift) % drawn.shape[longest]
        spots.append(tuple(where))
    return drawn.at[spots[0]].set(low).at[spots[1]].set(largest)


def block_scale(key, dims, cuts, low, top_value):
    level = 1.0
    for axis_at, shards_of in cuts:
        draws = jax.random.uniform(jax.random.fold_in(jax.random.fold_in(key, 6), axis_at), (shards_of,), jnp.float32, low / len(cuts), top_value / len(cuts))
        level = level * jnp.repeat(jnp.exp(draws), dims[axis_at] // shards_of).reshape((-1,) + (1,) * (len(dims) - 1 - axis_at))
    return level


def noise(stream_key, dims, scale, bound, cuts=(), held_as=jnp.bfloat16):
    values = scale * jax.random.normal(stream_key, dims, jnp.float32)
    if cuts:
        values = values * block_scale(stream_key, dims, cuts, -0.22, 0.18)
    return jnp.clip(values, -bound, bound).astype(held_as)


def setup_inputs(seed: int = 0) -> dict:
    key_of = jax.random.split(jax.random.key(seed), 17)
    inputs = noise(key_of[0], (SEQS, SLOTS, D), 1.0, 6.0, ((0, 32),))
    norm_first = jnp.clip(1.0 + 0.1 * jax.random.normal(key_of[1], (D,), jnp.float32), 0.5, 1.5).astype(jnp.bfloat16)
    w_query = noise(key_of[2], (D, INNER), (16 * D) ** -0.5, 0.046875, ((0, 32),))
    w_key = noise(key_of[3], (D, INNER), D ** -0.5, 0.1875, ((0, 32),))
    w_value = noise(key_of[4], (D, INNER), D ** -0.5, 0.1875, ((0, 32),))
    w_out = noise(key_of[5], (INNER, D), (INNER // 32) ** -0.5, 1.0, ((0, 32),))
    rel_table = noise(key_of[6], (HEADS * BUCKETS,), 1.0, 4.0, ((0, 32),))
    x_table = noise(key_of[7], (HEADS * BUCKETS,), 1.0, 4.0, ((0, 32),))
    y_table = noise(key_of[8], (HEADS * BUCKETS,), 1.0, 4.0, ((0, 32),))
    norm_second = jnp.clip(1.0 + 0.1 * jax.random.normal(key_of[9], (D,), jnp.float32), 0.5, 1.5).astype(jnp.bfloat16)
    w_gate = noise(key_of[10], (D, FF), D ** -0.5, 0.1875, ((0, 32),))
    w_up = noise(key_of[11], (D, FF), D ** -0.5, 0.1875, ((0, 32),))
    w_down = noise(key_of[12], (FF, D), FF ** -0.5, 0.109375, ((0, 32),))
    lengths = draw_lengths(jax.random.fold_in(key_of[16], 71), 0)
    boxes = touch_ends(jax.random.randint(key_of[14], (SEQS, 2, SLOTS), 0, 1001), jax.random.fold_in(key_of[14], 1), 0, 1000).astype(jnp.int32)
    cotangent = noise(key_of[15], (SEQS, SLOTS, D), 1.0, 6.0, ((0, 32),))
    return dict(inputs=inputs, norm_first=norm_first, w_query=w_query, w_key=w_key, w_value=w_value, w_out=w_out, rel_table=rel_table, x_table=x_table, y_table=y_table, norm_second=norm_second, w_gate=w_gate, w_up=w_up, w_down=w_down, lengths=lengths, boxes=boxes, cotangent=cotangent)


epsilon = 1e-06
coord_top = 1000
token_reach = 128
layout_reach = 256
masked_score = -1e+30
gelu_scale = 0.7978845608028654

@jax.custom_vjp
def low(v):
    return lax.optimization_barrier(v.astype(jnp.bfloat16)).astype(jnp.float32)

@jax.custom_vjp
def low_back(v):
    return v

def low_keep(v):
    return (low(v), None)

def low_pass(kept, grad):
    return (grad,)

def back_keep(v):
    return (v, None)

def back_low(kept, grad):
    return (low(grad),)
low.defvjp(low_keep, low_pass)
low_back.defvjp(back_keep, back_low)

def bucket_table(span, buckets, reach):
    offsets = np.arange(-span, span + 1)
    half = buckets // 2
    exact = half // 2
    side = np.where(offsets > 0, half, 0)
    distance = np.abs(offsets)
    safe = np.maximum(distance, 1)
    large = exact + (np.log(safe / exact) / np.log(reach / exact) * (half - exact)).astype(np.int64)
    large = np.minimum(large, half - 1)
    return side + np.where(distance < exact, distance, large)

def onehot_table(span, reach):
    table = bucket_table(span, BUCKETS, reach)
    return jnp.asarray(np.arange(BUCKETS)[:, None] == table[None, :]).astype(jnp.float32)

def widen(table, span, reach):
    return jnp.dot(table.reshape(HEADS, BUCKETS), onehot_table(span, reach), precision=lax.Precision.HIGHEST, preferred_element_type=jnp.float32)

def bias_of(vectors, box):
    rel_vector, x_vector, y_vector = vectors
    places = np.arange(SLOTS)
    token_index = jnp.asarray(places[None, :] - places[:, None] + SLOTS - 1).astype(jnp.int32)
    x_index = (box[0][None, :] - box[0][:, None] + coord_top).astype(jnp.int32)
    y_index = (box[1][None, :] - box[1][:, None] + coord_top).astype(jnp.int32)
    return jnp.take(rel_vector, token_index, axis=1) + jnp.take(x_vector, x_index, axis=1) + jnp.take(y_vector, y_index, axis=1)

def norm_apply(values, gain):
    return values * lax.rsqrt(lax.optimization_barrier(jnp.mean(values * values, axis=-1, keepdims=True)) + epsilon) * gain

def gate_apply(gate, upper):
    return 0.5 * gate * (1.0 + jnp.tanh(gelu_scale * (gate + 0.044715 * gate * gate * gate))) * upper

def matmul(left, right):
    return jnp.dot(left, right, precision=lax.Precision.HIGHEST, preferred_element_type=jnp.float32)

def block(inputs, norm_first, w_query, w_key, w_value, w_out, rel_table, x_table, y_table, norm_second, w_gate, w_up, w_down, lengths, boxes):
    seq_count = inputs.shape[0]
    inner_width = HEADS * HEAD_DIM
    rows = inputs.reshape(seq_count * SLOTS, D)
    normed_one = low(norm_apply(rows, norm_first))
    query = low_back(low(matmul(normed_one, w_query)))
    key_rows = low_back(low(matmul(normed_one, w_key)))
    value_rows = low_back(low(matmul(normed_one, w_value)))
    vectors = (widen(rel_table, SLOTS - 1, token_reach), widen(x_table, coord_top, layout_reach), widen(y_table, coord_top, layout_reach))

    def attend_one(packed):
        query_seq, key_seq, value_seq, length, box = packed
        bias = bias_of(vectors, box)
        heads_q = query_seq.reshape(SLOTS, HEADS, HEAD_DIM)
        heads_k = key_seq.reshape(SLOTS, HEADS, HEAD_DIM)
        heads_v = value_seq.reshape(SLOTS, HEADS, HEAD_DIM)
        scores = low_back(jnp.einsum('qhd,khd->hqk', heads_q, heads_k, precision=lax.Precision.HIGHEST)) + bias
        keep = jnp.arange(SLOTS) < length
        scores = jnp.where(keep[None, None, :], scores, masked_score)
        top = lax.optimization_barrier(jnp.max(scores, axis=-1, keepdims=True))
        weights = jnp.exp(scores - top)
        probs = weights / lax.optimization_barrier(jnp.sum(weights, axis=-1, keepdims=True))
        mixed_seq = jnp.einsum('hqk,khd->qhd', low(probs), heads_v, precision=lax.Precision.HIGHEST)
        return mixed_seq.reshape(SLOTS, inner_width)
    mixed = lax.map(jax.checkpoint(attend_one), (query.reshape(seq_count, SLOTS, inner_width), key_rows.reshape(seq_count, SLOTS, inner_width), value_rows.reshape(seq_count, SLOTS, inner_width), lengths, boxes))
    mixed = low_back(low(mixed.reshape(seq_count * SLOTS, inner_width)))
    hidden = rows + low_back(matmul(mixed, w_out))
    normed_two = low(norm_apply(hidden, norm_second))
    gate = low_back(matmul(normed_two, w_gate))
    upper = low_back(matmul(normed_two, w_up))
    activated = low(gate_apply(gate, upper))
    return (hidden + matmul(activated, w_down)).reshape(seq_count, SLOTS, D)

def reference(inputs, norm_first, w_query, w_key, w_value, w_out, rel_table, x_table, y_table, norm_second, w_gate, w_up, w_down, lengths, boxes, cotangent):
    floats = [value.astype(jnp.float32) for value in (inputs, norm_first, w_query, w_key, w_value, w_out, rel_table, x_table, y_table, norm_second, w_gate, w_up, w_down)]

    def forward(*values):
        return block(*values, lengths, boxes)
    result, pull = jax.vjp(forward, *floats)
    grads = pull(cotangent.astype(jnp.float32))
    return (result.astype(jnp.bfloat16), grads[0], grads[1], grads[2], grads[3], grads[4], grads[5], grads[6], grads[7], grads[8], grads[9], grads[10], grads[11], grads[12])
```

```python
import functools

import jax
import jax.numpy as jnp
import numpy as np
from jax import lax
from jax.experimental import pallas as pl
from jax.experimental.pallas import tpu as pltpu
from jax.sharding import PartitionSpec as P

HEADS = 16
HEAD_DIM = 64
BUCKETS = 32
AXES = ("wide", "narrow")

epsilon = 1e-06
coord_top = 1000
token_reach = 128
layout_reach = 256
masked_score = -1e30
gelu_scale = 0.7978845608028654

VMEM_LIMIT = 60 * 2**20
ROW_TILE = 256
STRIP = 16
BIAS_TILE = 128
DEAD_BUCKET = 16
CORE_BIT = 1


def params_for(flops, moved):
    return dict(
        compiler_params=pltpu.CompilerParams(vmem_limit_bytes=VMEM_LIMIT),
        cost_estimate=pl.CostEstimate(
            flops=int(flops), bytes_accessed=int(moved), transcendentals=0
        ),
    )


def bucket_table(span, buckets, reach):
    offsets = np.arange(-span, span + 1)
    half = buckets // 2
    exact = half // 2
    side = np.where(offsets > 0, half, 0)
    distance = np.abs(offsets)
    safe = np.maximum(distance, 1)
    large = exact + (np.log(safe / exact) / np.log(reach / exact) * (half - exact)).astype(np.int64)
    large = np.minimum(large, half - 1)
    return side + np.where(distance < exact, distance, large)


def magnitude_steps(span, reach):
    half = BUCKETS // 2
    exact = half // 2
    offsets = np.arange(span + 1)
    table = bucket_table(span, BUCKETS, reach)[span:]
    magnitude = table - np.where(offsets > 0, half, 0)
    steps = []
    for level in range(exact + 1, half):
        if (magnitude >= level).any():
            steps.append(int(np.argmax(magnitude >= level)))
    return steps


def bucket_index(offset, span, reach):
    half = BUCKETS // 2
    exact = half // 2
    distance = jnp.abs(offset)
    magnitude = jnp.minimum(distance, exact)
    for edge in magnitude_steps(span, reach):
        magnitude = magnitude + (distance >= edge).astype(jnp.int32)
    return magnitude + jnp.where(offset > 0, half, 0)


def rel_marks(slots, zero):
    places = np.arange(slots)
    offset = np.where(places < 768, places - zero, -300)
    table = bucket_table(slots - 1, BUCKETS, token_reach)
    return table[offset + slots - 1][None, :] == np.arange(BUCKETS)[:, None]


def write_marks(marks_ref, x_tile, y_tile):
    one = jnp.ones(x_tile.shape, jnp.bfloat16)
    zero = jnp.zeros(x_tile.shape, jnp.bfloat16)
    for b in range(BUCKETS):
        marks_ref[b * 16 : b * 16 + 16, :] = jnp.where(x_tile == b, one, zero)
        marks_ref[512 + b * 16 : 512 + b * 16 + 16, :] = jnp.where(y_tile == b, one, zero)


def index_kernel(len_ref, box_ref, turned_ref, ix_ref, iy_ref):
    place = lax.broadcasted_iota(jnp.int32, ix_ref.shape, 1)
    x_bucket = bucket_index(box_ref[0:1, :] - turned_ref[:, 0:1], coord_top, layout_reach)
    y_bucket = bucket_index(box_ref[1:2, :] - turned_ref[:, 1:2], coord_top, layout_reach)
    x_bucket = jnp.where(place < len_ref[0], x_bucket, DEAD_BUCKET)
    ix_ref[...] = x_bucket.astype(jnp.float32).astype(jnp.bfloat16)
    iy_ref[...] = y_bucket.astype(jnp.float32).astype(jnp.bfloat16)


def index_call(length, box):
    slots = box.shape[1]
    tile = pl.BlockSpec((BIAS_TILE, slots), lambda i: (i, 0))
    return pl.pallas_call(
        index_kernel,
        grid=(slots // BIAS_TILE,),
        in_specs=[
            pl.BlockSpec(memory_space=pltpu.SMEM),
            pl.BlockSpec((2, slots), lambda i: (0, 0)),
            pl.BlockSpec((BIAS_TILE, 2), lambda i: (i, 0)),
        ],
        out_specs=[tile, tile],
        out_shape=[jax.ShapeDtypeStruct((slots, slots), jnp.bfloat16)] * 2,
        name="index",
        **params_for(1e9, 4e6),
    )(length, box, box.T)


def prepare_kernel(tables_ref, marks_ref, lhs_ref, skew_ref):
    slots = marks_ref.shape[1]
    tables = tables_ref[...]
    rel_row = jnp.dot(
        tables[:, :BUCKETS], marks_ref[...], preferred_element_type=jnp.float32
    )
    for h in range(HEADS):
        wide = jnp.broadcast_to(rel_row[h : h + 1, :], (BIAS_TILE, slots))
        skew_ref[h] = pltpu.roll(wide, 0, 1, stride=1, stride_axis=0)[:, :640]
    tall, long = HEADS * 16, 2 * BUCKETS * 16
    layout = tables[:, BUCKETS:]
    dead = lax.broadcasted_iota(jnp.int32, layout.shape, 1) == DEAD_BUCKET
    layout = jnp.where(dead, jnp.asarray(masked_score, jnp.bfloat16), layout)
    head_of = lax.broadcasted_iota(jnp.int32, (tall, HEADS), 0) // 16
    pick_head = head_of == lax.broadcasted_iota(jnp.int32, (tall, HEADS), 1)
    bucket_of = lax.broadcasted_iota(jnp.int32, (2 * BUCKETS, long), 1) // 16
    pick_bucket = bucket_of == lax.broadcasted_iota(jnp.int32, (2 * BUCKETS, long), 0)
    by_head = jnp.dot(
        pick_head.astype(jnp.bfloat16), layout, preferred_element_type=jnp.float32
    ).astype(jnp.bfloat16)
    full = jnp.dot(
        by_head, pick_bucket.astype(jnp.bfloat16), preferred_element_type=jnp.float32
    )
    same = (
        lax.broadcasted_iota(jnp.int32, (tall, long), 0) % 16
        == lax.broadcasted_iota(jnp.int32, (tall, long), 1) % 16
    )
    lhs_ref[...] = jnp.where(same, full, 0.0).astype(jnp.bfloat16)


def prepare_call(tables, slots):
    return pl.pallas_call(
        prepare_kernel,
        out_shape=[
            jax.ShapeDtypeStruct((HEADS * 16, 2 * BUCKETS * 16), jnp.bfloat16),
            jax.ShapeDtypeStruct((HEADS, BIAS_TILE, 640), jnp.float32),
        ],
        name="prepare",
        **params_for(1e9, 6e6),
    )(tables, jnp.asarray(rel_marks(slots, 256)).astype(jnp.bfloat16))


def bias_kernel(first, ix_ref, iy_ref, lhs_ref, skew_ref, *rest):
    bias_ref, marks_ref = rest[-2:]
    block = pl.program_id(0) + first
    slots = ix_ref.shape[1]

    def body(t, carry):
        r0 = pl.multiple_of(t * 16, 16)
        write_marks(marks_ref, ix_ref[pl.ds(r0, 16), :], iy_ref[pl.ds(r0, 16), :])
        out = jnp.dot(lhs_ref[...], marks_ref[...], preferred_element_type=jnp.float32)
        for c in range(slots // 128):
            shift = pl.multiple_of((jnp.clip(c - block, -2, 2) + 2) * 128, 128)
            cols = slice(c * 128, c * 128 + 128)
            for h in range(HEADS):
                bias_ref[h, pl.ds(r0, 16), cols] = (
                    out[h * 16 : h * 16 + 16, cols]
                    + skew_ref[h, pl.ds(r0, 16), pl.ds(shift, 128)]
                )
        return carry

    lax.fori_loop(0, BIAS_TILE // 16, body, 0)


def bias_call(ix, iy, lhs, skew, begin, end, held=None):
    slots = ix.shape[0]
    tile = pl.BlockSpec((BIAS_TILE, slots), lambda i: (i + begin, 0))
    in_specs = [
        tile,
        tile,
        pl.BlockSpec(lhs.shape, lambda i: (0, 0)),
        pl.BlockSpec(skew.shape, lambda i: (0, 0, 0)),
    ]
    args = [ix, iy, lhs, skew]
    aliases = {}
    if held is not None:
        in_specs.append(pl.BlockSpec(memory_space=pl.ANY))
        args.append(held)
        aliases = {4: 0}
    share = (end - begin) * BIAS_TILE / slots
    return pl.pallas_call(
        functools.partial(bias_kernel, begin),
        grid=(end - begin,),
        in_specs=in_specs,
        out_specs=pl.BlockSpec((HEADS, BIAS_TILE, slots), lambda i: (0, i + begin, 0)),
        out_shape=jax.ShapeDtypeStruct((HEADS, slots, slots), jnp.float32),
        scratch_shapes=[pltpu.VMEM((2 * BUCKETS * 16, slots), jnp.bfloat16)],
        input_output_aliases=aliases,
        name="bias",
        **params_for(34e9 * share, 72e6 * share),
    )(*args)


def own_lanes(h):
    left = lax.broadcasted_iota(jnp.int32, (1, 128), 1) < HEAD_DIM
    return left if h == 0 else jnp.logical_not(left)


def attend_kernel(q_ref, k_ref, v_ref, bias_ref, probs_ref, mixed_ref):
    q, k, v = q_ref[...], k_ref[...], v_ref[...]
    outs = []
    for h in range(2):
        q_own = jnp.where(own_lanes(h), q, jnp.zeros_like(q))
        scores = lax.dot_general(
            q_own, k, (((1,), (1,)), ((), ())), preferred_element_type=jnp.float32
        )
        strips = []
        for r in range(0, q.shape[0], STRIP):
            strip = scores[r : r + STRIP] + bias_ref[h, r : r + STRIP, :]
            top = jnp.max(strip, axis=1, keepdims=True)
            weights = jnp.exp(strip - top)
            total = jnp.sum(weights, axis=1, keepdims=True)
            strips.append((weights * (1.0 / total)).astype(jnp.bfloat16))
        probs = jnp.concatenate(strips, axis=0)
        probs_ref[h] = probs
        outs.append(jnp.dot(probs, v, preferred_element_type=jnp.float32))
    mixed_ref[...] = jnp.where(own_lanes(0), outs[0], outs[1]).astype(jnp.bfloat16)


def attend_call(query, key_rows, value_rows, bias):
    slots, inner = query.shape
    pairs = inner // 128
    tile = min(ROW_TILE, slots)
    rows = pl.BlockSpec((tile, 128), lambda p, i: (i, p))
    square = pl.BlockSpec((2, tile, slots), lambda p, i: (p, i, 0))
    return pl.pallas_call(
        attend_kernel,
        grid=(pairs, slots // tile),
        in_specs=[
            rows,
            pl.BlockSpec((slots, 128), lambda p, i: (0, p)),
            pl.BlockSpec((slots, 128), lambda p, i: (0, p)),
            square,
        ],
        out_specs=[square, rows],
        out_shape=[
            jax.ShapeDtypeStruct((HEADS, slots, slots), jnp.bfloat16),
            jax.ShapeDtypeStruct((slots, inner), jnp.bfloat16),
        ],
        name="attend",
        **params_for(34e9, 100e6),
    )(query, key_rows, value_rows, bias)


def attend_back_kernel(q_ref, k_ref, v_ref, grad_ref, probs_ref, *rest):
    ds_ref, dq_ref, dk_ref, dv_ref, k_sum, v_sum = rest[-6:]
    step = pl.program_id(1)
    q, k, v, grad = q_ref[...], k_ref[...], v_ref[...], grad_ref[...]
    q_turned, grad_turned = q.T, grad.T

    @pl.when(step == 0)
    def _():
        k_sum[...] = jnp.zeros_like(k_sum)
        v_sum[...] = jnp.zeros_like(v_sum)

    outs = []
    for h in range(2):
        grad_own = jnp.where(own_lanes(h), grad, jnp.zeros_like(grad))
        grad_probs = lax.dot_general(
            grad_own, v, (((1,), (1,)), ((), ())), preferred_element_type=jnp.float32
        )
        strips = []
        for r in range(0, q.shape[0], STRIP):
            probs = probs_ref[h, r : r + STRIP, :].astype(jnp.float32)
            terms = probs * grad_probs[r : r + STRIP]
            delta = jnp.sum(terms, axis=1, keepdims=True)
            strips.append((terms - probs * delta).astype(jnp.bfloat16))
        ds = jnp.concatenate(strips, axis=0)
        ds_ref[h] = ds
        outs.append(jnp.dot(ds, k, preferred_element_type=jnp.float32))
        own = slice(h * HEAD_DIM, (h + 1) * HEAD_DIM)
        k_sum[own, :] += jnp.dot(q_turned[own], ds, preferred_element_type=jnp.float32)
        v_sum[own, :] += jnp.dot(
            grad_turned[own], probs_ref[h], preferred_element_type=jnp.float32
        )
    dq_ref[...] = jnp.where(own_lanes(0), outs[0], outs[1]).astype(jnp.bfloat16)

    @pl.when(step == pl.num_programs(1) - 1)
    def _():
        dk_ref[...] = k_sum[...].T.astype(jnp.bfloat16)
        dv_ref[...] = v_sum[...].T.astype(jnp.bfloat16)


def attend_back_call(query, key_rows, value_rows, grad_mixed, probs, begin, end, held=None):
    slots, inner = query.shape
    tile = min(ROW_TILE, slots)
    rows = pl.BlockSpec((tile, 128), lambda p, i: (i, p + begin))
    whole = pl.BlockSpec((slots, 128), lambda p, i: (0, p + begin))
    square = pl.BlockSpec((2, tile, slots), lambda p, i: (p + begin, i, 0))
    args = [query, key_rows, value_rows, grad_mixed, probs]
    in_specs = [rows, whole, whole, rows, square]
    aliases = {}
    if held is not None:
        aliases = {len(args) + at: at for at in range(len(held))}
        in_specs += [pl.BlockSpec(memory_space=pl.ANY)] * len(held)
        args += list(held)
    share = (end - begin) * 128 / inner
    return pl.pallas_call(
        attend_back_kernel,
        grid=(end - begin, slots // tile),
        in_specs=in_specs,
        out_specs=[square, rows, whole, whole],
        out_shape=[jax.ShapeDtypeStruct((HEADS, slots, slots), jnp.bfloat16)]
        + [jax.ShapeDtypeStruct((slots, inner), jnp.bfloat16)] * 3,
        scratch_shapes=[pltpu.VMEM((128, slots), jnp.float32)] * 2,
        input_output_aliases=aliases,
        name="attend_back",
        **params_for(34e9 * share, 72e6 * share),
    )(*args)


def table_kernel(
    first, ds_ref, ix_ref, iy_ref, layout_ref, rel_ref, layout_sum, rel_sum, marks_ref
):
    step = pl.program_id(0)
    block = step + first
    slots = ix_ref.shape[1]

    @pl.when(step == 0)
    def _():
        layout_sum[...] = jnp.zeros_like(layout_sum)
        rel_sum[...] = jnp.zeros_like(rel_sum)

    def body(t, carry):
        r0 = pl.multiple_of(t * 16, 16)
        write_marks(marks_ref, ix_ref[pl.ds(r0, 16), :], iy_ref[pl.ds(r0, 16), :])
        ds = ds_ref[:, pl.ds(r0, 16), :].reshape(HEADS * 16, slots)
        layout_sum[...] += lax.dot_general(
            marks_ref[...], ds, (((1,), (1,)), ((), ())), preferred_element_type=jnp.float32
        )
        for c in range(slots // 128):
            shift = pl.multiple_of((jnp.clip(c - block, -2, 2) + 2) * 128, 128)
            cols = slice(c * 128, c * 128 + 128)
            for h in range(HEADS):
                rel_sum[h, pl.ds(r0, 16), pl.ds(shift, 128)] += ds_ref[
                    h, pl.ds(r0, 16), cols
                ].astype(jnp.float32)
        return carry

    lax.fori_loop(0, BIAS_TILE // 16, body, 0)

    @pl.when(step == pl.num_programs(0) - 1)
    def _():
        shape = layout_sum.shape
        same = (
            lax.broadcasted_iota(jnp.int32, shape, 0) % 16
            == lax.broadcasted_iota(jnp.int32, shape, 1) % 16
        )
        kept = jnp.where(same, layout_sum[...], 0.0)
        layout_ref[...] = kept.reshape(2 * BUCKETS, 16, HEADS * 16).sum(axis=1)
        tall = (BIAS_TILE, BIAS_TILE)
        flip = (
            lax.broadcasted_iota(jnp.int32, tall, 0) + lax.broadcasted_iota(jnp.int32, tall, 1)
            == BIAS_TILE - 1
        ).astype(jnp.float32)
        for h in range(HEADS):
            upside = jnp.dot(
                flip,
                rel_sum[h],
                precision=lax.Precision.HIGHEST,
                preferred_element_type=jnp.float32,
            )
            padded = jnp.concatenate(
                [upside, jnp.zeros((BIAS_TILE, slots - 640), jnp.float32)], axis=1
            )
            back = pltpu.roll(padded, 0, 1, stride=1, stride_axis=0)
            rel_ref[h : h + 1, :] = jnp.sum(back, axis=0, keepdims=True)


def table_call(ds, ix, iy, begin, end):
    slots = ix.shape[0]
    tile = pl.BlockSpec((BIAS_TILE, slots), lambda i: (i + begin, 0))
    share = (end - begin) * BIAS_TILE / slots
    return pl.pallas_call(
        functools.partial(table_kernel, begin),
        grid=(end - begin,),
        in_specs=[
            pl.BlockSpec((HEADS, BIAS_TILE, slots), lambda i: (0, i + begin, 0)),
            tile,
            tile,
        ],
        out_specs=[
            pl.BlockSpec((2 * BUCKETS, HEADS * 16), lambda i: (0, 0)),
            pl.BlockSpec((HEADS, slots), lambda i: (0, 0)),
        ],
        out_shape=[
            jax.ShapeDtypeStruct((2 * BUCKETS, HEADS * 16), jnp.float32),
            jax.ShapeDtypeStruct((HEADS, slots), jnp.float32),
        ],
        scratch_shapes=[
            pltpu.VMEM((2 * BUCKETS * 16, HEADS * 16), jnp.float32),
            pltpu.VMEM((HEADS, BIAS_TILE, 640), jnp.float32),
            pltpu.VMEM((2 * BUCKETS * 16, slots), jnp.bfloat16),
        ],
        name="table_back",
        **params_for(34e9 * share, 36e6 * share),
    )(ds, ix, iy)


def table_finish(parts, slots):
    layout = sum(part[0] for part in parts)
    rel = sum(part[1] for part in parts)
    layout = layout.reshape(2 * BUCKETS, HEADS, 16).sum(axis=2).T
    rel = lax.dot_general(
        rel,
        jnp.asarray(rel_marks(slots, 383)).astype(jnp.float32),
        (((1,), (1,)), ((), ())),
        precision=lax.Precision.HIGHEST,
        preferred_element_type=jnp.float32,
    )
    return rel, layout[:, :BUCKETS], layout[:, BUCKETS:]


def ffn_kernel(
    n_ref, turned_ref, seed_ref, hidden_ref, gate_ref, up_ref, down_ref,
    out_ref, dn_ref, dgate_ref, dup_ref, ddown_ref, out_sum, dn_sum,
):
    step = pl.program_id(0)

    @pl.when(step == 0)
    def _():
        out_sum[...] = hidden_ref[...]
        dn_sum[...] = jnp.zeros_like(dn_sum)

    seed = seed_ref[...]
    w_gate, w_up, w_down = gate_ref[...], up_ref[...], down_ref[...]
    gate = jnp.dot(n_ref[...], w_gate, preferred_element_type=jnp.float32)
    upper = jnp.dot(n_ref[...], w_up, preferred_element_type=jnp.float32)
    grad_act = lax.dot_general(
        seed, w_down, (((1,), (1,)), ((), ())), preferred_element_type=jnp.float32
    )
    square = gate * gate
    tanh = jnp.tanh(gelu_scale * (gate + 0.044715 * gate * square))
    cdf = 0.5 * (1.0 + tanh)
    gelu = gate * cdf
    slope = cdf + 0.5 * gate * (1.0 - tanh * tanh) * gelu_scale * (1.0 + 3 * 0.044715 * square)
    activated = (gelu * upper).astype(jnp.bfloat16)
    grad_gate = (grad_act * upper * slope).astype(jnp.bfloat16)
    grad_upper = (grad_act * gelu).astype(jnp.bfloat16)
    out_sum[...] += jnp.dot(activated, w_down, preferred_element_type=jnp.float32)
    dn_sum[...] += lax.dot_general(
        grad_gate, w_gate, (((1,), (1,)), ((), ())), preferred_element_type=jnp.float32
    ) + lax.dot_general(
        grad_upper, w_up, (((1,), (1,)), ((), ())), preferred_element_type=jnp.float32
    )
    dgate_ref[...] = jnp.dot(
        turned_ref[...], grad_gate, preferred_element_type=jnp.float32
    ).astype(jnp.bfloat16)
    dup_ref[...] = jnp.dot(
        turned_ref[...], grad_upper, preferred_element_type=jnp.float32
    ).astype(jnp.bfloat16)
    ddown_ref[...] = lax.dot_general(
        activated, seed, (((0,), (0,)), ((), ())), preferred_element_type=jnp.float32
    ).astype(jnp.bfloat16)

    @pl.when(step == pl.num_programs(0) - 1)
    def _():
        out_ref[...] = out_sum[...].astype(jnp.bfloat16)
        dn_ref[...] = dn_sum[...]


def ffn_call(normed, turned, seed, hidden, packed, first, w_down):
    slots, width = normed.shape
    ff = w_down.shape[0]
    tile = 256
    count = ff // tile
    full = pl.BlockSpec((slots, width), lambda f: (0, 0))
    turned_full = pl.BlockSpec((width, slots), lambda f: (0, 0))
    column = pl.BlockSpec((width, tile), lambda f: (0, f))
    return pl.pallas_call(
        ffn_kernel,
        grid=(count,),
        in_specs=[
            full,
            turned_full,
            full,
            full,
            pl.BlockSpec((width, tile), lambda f: (0, f + first)),
            pl.BlockSpec((width, tile), lambda f: (0, f + first + count)),
            pl.BlockSpec((tile, width), lambda f: (f, 0)),
        ],
        out_specs=[full, full, column, column, pl.BlockSpec((tile, width), lambda f: (f, 0))],
        out_shape=[
            jax.ShapeDtypeStruct((slots, width), jnp.bfloat16),
            jax.ShapeDtypeStruct((slots, width), jnp.float32),
            jax.ShapeDtypeStruct((width, ff), jnp.bfloat16),
            jax.ShapeDtypeStruct((width, ff), jnp.bfloat16),
            jax.ShapeDtypeStruct((ff, width), jnp.bfloat16),
        ],
        scratch_shapes=[pltpu.VMEM((slots, width), jnp.float32)] * 2,
        name="ffn",
        **params_for(18 * slots * width * ff, 50e6),
    )(normed, turned, seed, hidden, packed, packed, w_down)


def unpack_kernel(down_rows, part_rows, packed_ref, out_ref):
    width = out_ref.shape[1]
    for at in range(out_ref.shape[0] // down_rows):
        for group in range(-(-down_rows // part_rows)):
            count = min(part_rows, down_rows - group * part_rows)
            here = at * down_rows + group * part_rows
            out_ref[here : here + count, :] = packed_ref[
                at * part_rows : at * part_rows + count, group * width : (group + 1) * width
            ]


def unpack_call(packed, first, down_rows, part_rows, width):
    count = packed.shape[0] // part_rows
    groups = -(-down_rows // part_rows)
    joint = 1
    while (joint * down_rows) % 16 or (joint * part_rows) % 16:
        joint *= 2
    return pl.pallas_call(
        functools.partial(unpack_kernel, down_rows, part_rows),
        grid=(count // joint,),
        in_specs=[
            pl.BlockSpec(
                (joint * part_rows, groups * width), lambda d: (d, first // (groups * width))
            )
        ],
        out_specs=pl.BlockSpec((joint * down_rows, width), lambda d: (d, 0)),
        out_shape=jax.ShapeDtypeStruct((count * down_rows, width), jnp.bfloat16),
        name="unpack",
        **params_for(1e6, 12e6),
    )(packed)


class Exchange:
    def __init__(self, mesh):
        self.count = mesh.shape["wide"] * mesh.shape["narrow"]
        self.bits = self.count.bit_length() - 1
        assert self.count == 1 << self.bits
        one, two, three, *tail = [b for b in range(self.bits) if b != CORE_BIT]
        self.orders = (
            [CORE_BIT, one, two] + tail + [three],
            [CORE_BIT, two, three, one] + tail,
            [CORE_BIT, three, one, two] + tail,
        )

    def mine(self, bit):
        return (lax.axis_index(AXES) >> bit) & 1

    def swap(self, value, bit):
        pairs = [(d, d ^ (1 << bit)) for d in range(self.count)]
        return lax.ppermute(value, AXES, pairs)

    def spread(self, shard):
        copies = jnp.broadcast_to(shard[None, :], (self.count, shard.shape[0]))
        return lax.all_to_all(copies, AXES, 0, 0, tiled=True)

    def sum_small(self, terms):
        return jnp.sum(lax.all_to_all(terms, AXES, 0, 0, tiled=True), axis=0)


class Gather:
    def __init__(self, exchange, shard, order):
        self.exchange = exchange
        self.value = shard
        self.steps = list(reversed(exchange.orders[order]))
        self.held = []
        self.flight = None

    def done(self):
        return not self.steps

    def go(self):
        self.flight = self.exchange.swap(self.value, self.steps[0])

    def land(self):
        bit = self.steps.pop(0)
        other, self.flight = self.flight, None
        spot = sum(b > bit for b in self.held)
        high = self.exchange.mine(bit) == 1
        self.value = jnp.stack(
            [jnp.where(high, other, self.value), jnp.where(high, self.value, other)], axis=spot
        )
        self.held.append(bit)


class Scatter:
    def __init__(self, exchange, terms, order):
        self.exchange = exchange
        rows = terms.shape[0] // exchange.count
        self.value = terms.reshape((2,) * exchange.bits + (rows,) + terms.shape[1:])
        self.steps = list(exchange.orders[order])
        self.held = list(range(exchange.bits - 1, -1, -1))
        self.flight = None

    def done(self):
        return not self.steps

    def go(self):
        bit = self.steps[0]
        self.spot = self.held.index(bit)
        away = lax.dynamic_index_in_dim(
            self.value, 1 - self.exchange.mine(bit), self.spot, keepdims=False
        )
        self.flight = self.exchange.swap(away, bit)

    def land(self):
        bit = self.steps.pop(0)
        other, self.flight = self.flight, None
        stay = lax.dynamic_index_in_dim(
            self.value, self.exchange.mine(bit), self.spot, keepdims=False
        )
        value = stay.astype(jnp.float32) + other.astype(jnp.float32)
        if self.steps:
            value = value.astype(jnp.bfloat16)
        self.value = value
        self.held.pop(self.spot)


class Traffic:
    limit = 5

    def __init__(self):
        self.tasks = []

    def add(self, *tasks):
        self.tasks += tasks
        self.send()

    def send(self):
        busy = sum(task.flight is not None for task in self.tasks)
        for task in self.tasks:
            if task.flight is None and busy < self.limit:
                task.go()
                busy += 1

    def step(self, *work):
        flying = [task for task in self.tasks if task.flight is not None]
        work, flights = lax.optimization_barrier((work, [task.flight for task in flying]))
        for task, flight in zip(flying, flights):
            task.flight = flight
            task.land()
        self.tasks = [task for task in self.tasks if not task.done()]
        self.send()
        return work[0] if len(work) == 1 else work


def norm_apply(values, gain):
    return values * lax.rsqrt(jnp.mean(values * values, axis=-1, keepdims=True) + epsilon) * gain


def plain_product(left, right):
    return jnp.dot(left, right, preferred_element_type=jnp.float32)


def left_transposed(left, right):
    return lax.dot_general(
        left, right, (((0,), (0,)), ((), ())), preferred_element_type=jnp.float32
    )


def right_transposed(left, right):
    return lax.dot_general(
        left, right, (((1,), (1,)), ((), ())), preferred_element_type=jnp.float32
    )


def layer(
    exchange, inputs, norm_first, w_query, w_key, w_value, w_out, rel_table, x_table, y_table,
    norm_second, w_gate, w_up, w_down, lengths, boxes, cotangent,
):
    seq_count, slots, width = inputs.shape
    inner = w_query.shape[1]
    count = exchange.count
    entries = rel_table.shape[0]
    span = norm_first.shape[0]

    rows = inputs.reshape(slots, width).astype(jnp.float32)
    seed = cotangent.reshape(slots, width)
    traffic = Traffic()
    qkv_tasks = [
        Gather(exchange, shard, order) for order, shard in enumerate((w_query, w_key, w_value))
    ]
    traffic.add(*qkv_tasks)
    small = exchange.spread(
        jnp.concatenate([norm_first, norm_second, rel_table, x_table, y_table])
    )
    down_rows, part_rows = w_down.shape[0], w_out.shape[0]
    groups = -(-down_rows // part_rows)
    down_pad = jnp.pad(w_down, ((0, groups * part_rows - down_rows), (0, 0)))
    down_pad = [down_pad[at * part_rows : (at + 1) * part_rows] for at in range(groups)]
    packed = lax.all_gather(
        jnp.concatenate(down_pad + [w_out, w_gate, w_up], axis=1), AXES, axis=0, tiled=True
    )
    ix, iy = index_call(lengths, boxes[0])
    gain_one = small[:, :span].reshape(-1).astype(jnp.float32)
    gain_two = small[:, span : 2 * span].reshape(-1).astype(jnp.float32)
    tables = jnp.concatenate(
        [
            small[:, 2 * span + at * entries : 2 * span + (at + 1) * entries].reshape(
                HEADS, BUCKETS
            )
            for at in range(3)
        ],
        axis=1,
    )
    lhs, skew = prepare_call(tables, slots)
    blocks = slots // BIAS_TILE
    pieces = exchange.bits - 1
    bias = None
    for piece in range(pieces):
        begin, end = piece * blocks // pieces, (piece + 1) * blocks // pieces
        if bias is None:
            lhs = traffic.step(lhs)
        else:
            lhs, bias = traffic.step(lhs, bias)
        if end > begin:
            bias = bias_call(ix, iy, lhs, skew, begin, end, bias)
    normed_one = norm_apply(rows, gain_one).astype(jnp.bfloat16)
    normed_one, bias = traffic.step(normed_one, bias)
    query_full, key_full, value_full = (
        task.value.reshape(-1, task.value.shape[-1]) for task in qkv_tasks
    )
    query = plain_product(normed_one, query_full).astype(jnp.bfloat16)
    key_rows = plain_product(normed_one, key_full).astype(jnp.bfloat16)
    value_rows = plain_product(normed_one, value_full).astype(jnp.bfloat16)
    probs, mixed = attend_call(query, key_rows, value_rows, bias)
    first = groups * width
    out_full = packed[:, first : first + width]
    down_full = unpack_call(packed, 0, down_rows, part_rows, width)
    hidden = rows + plain_product(mixed, out_full)
    normed_two = norm_apply(hidden, gain_two).astype(jnp.bfloat16)
    output, grad_normed_two, d_gate, d_up, d_down = ffn_call(
        normed_two, normed_two.T, seed, hidden, packed, (first + width) // 256, down_full
    )
    ffn_tasks = [Scatter(exchange, part, at) for at, part in enumerate((d_gate, d_up, d_down))]
    traffic.add(*ffn_tasks)
    unused_two, norm_two_pull = jax.vjp(norm_apply, hidden, gain_two)
    hidden_part, grad_gain_two = norm_two_pull(grad_normed_two)
    grad_hidden = seed.astype(jnp.float32) + hidden_part
    branch_low = grad_hidden.astype(jnp.bfloat16)
    d_out = left_transposed(mixed, branch_low).astype(jnp.bfloat16)
    grad_mixed = right_transposed(branch_low, out_full).astype(jnp.bfloat16)
    grad_mixed, d_out = traffic.step(grad_mixed, d_out)
    out_task = Scatter(exchange, d_out, 0)
    traffic.add(out_task)
    pairs = inner // 128
    cuts = (0, pairs // 2, pairs)
    back = None
    for begin, end in zip(cuts[:-1], cuts[1:]):
        back = attend_back_call(
            query, key_rows, value_rows, grad_mixed, probs, begin, end, back
        )
        back = traffic.step(back)
    ds, dq, dk, dv = back
    d_weights = [left_transposed(normed_one, part).astype(jnp.bfloat16) for part in (dq, dk, dv)]
    dq, d_weights = traffic.step(dq, d_weights)
    w_tasks = [Scatter(exchange, part, at) for at, part in enumerate(d_weights)]
    traffic.add(*w_tasks)
    grad_normed_one = (
        right_transposed(dq, query_full)
        + right_transposed(dk, key_full)
        + right_transposed(dv, value_full)
    )
    unused_one, norm_one_pull = jax.vjp(norm_apply, rows, gain_one)
    rows_part, grad_gain_one = norm_one_pull(grad_normed_one)
    grad_inputs = (grad_hidden + rows_part).reshape(inputs.shape)
    parts = []
    pieces = 3
    grad_inputs, ix = traffic.step(grad_inputs, ix)
    for piece in range(pieces):
        begin, end = piece * blocks // pieces, (piece + 1) * blocks // pieces
        parts.append(table_call(ds, ix, iy, begin, end))
        ix, parts = traffic.step(ix, parts)
    grad_rel, grad_x, grad_y = table_finish(parts, slots)
    g_small = exchange.sum_small(
        jnp.concatenate(
            [
                part.reshape(count, -1)
                for part in (grad_gain_one, grad_gain_two, grad_rel, grad_x, grad_y)
            ],
            axis=1,
        )
    )
    while traffic.tasks:
        g_small = traffic.step(g_small)
    g_gate, g_up, g_down = (task.value for task in ffn_tasks)
    edges = [0, span, 2 * span, 2 * span + entries, 2 * span + 2 * entries, g_small.shape[0]]
    g_small = [g_small[a:b] for a, b in zip(edges[:-1], edges[1:])]
    return (
        output.reshape(inputs.shape),
        grad_inputs,
        g_small[0],
        w_tasks[0].value,
        w_tasks[1].value,
        w_tasks[2].value,
        out_task.value,
        g_small[2],
        g_small[3],
        g_small[4],
        g_small[1],
        g_gate,
        g_up,
        g_down,
    )


def solution(mesh):
    exchange = Exchange(mesh)
    vector, matrix, cube = P(AXES), P(AXES, None), P(AXES, None, None)
    in_specs = (
        (cube, vector)
        + (matrix,) * 4
        + (vector,) * 4
        + (matrix,) * 3
        + (vector, cube, cube)
    )
    out_specs = (cube, cube, vector) + (matrix,) * 4 + (vector,) * 4 + (matrix,) * 3

    def local(*args):
        return layer(exchange, *args)

    return jax.shard_map(local, mesh=mesh, in_specs=in_specs, out_specs=out_specs, check_vma=False)
```

```python
import functools

import jax
import jax.numpy as jnp
import numpy as np
from jax import lax
from jax.experimental import pallas as pl
from jax.experimental.pallas import tpu as pltpu
from jax.sharding import PartitionSpec as P

HEADS = 16
HEAD_DIM = 64
BUCKETS = 32
AXES = ("wide", "narrow")

epsilon = 1e-06
coord_top = 1000
token_reach = 128
layout_reach = 256
masked_score = -1e30
gelu_scale = 0.7978845608028654

VMEM_LIMIT = 60 * 2**20
ROW_TILE = 1024
STRIP = 16
BIAS_TILE = 128
DEAD_BUCKET = 16
CORE_BIT = 1
TABLE_JOINT = 4


def params_for(flops, moved):
    return dict(
        compiler_params=pltpu.CompilerParams(vmem_limit_bytes=VMEM_LIMIT),
        cost_estimate=pl.CostEstimate(
            flops=int(flops), bytes_accessed=int(moved), transcendentals=0
        ),
    )


def plain_product(left, right):
    return jnp.dot(left, right, preferred_element_type=jnp.float32)


def left_transposed(left, right):
    return lax.dot_general(
        left, right, (((0,), (0,)), ((), ())), preferred_element_type=jnp.float32
    )


def right_transposed(left, right):
    return lax.dot_general(
        left, right, (((1,), (1,)), ((), ())), preferred_element_type=jnp.float32
    )


def bucket_table(span, buckets, reach):
    offsets = np.arange(-span, span + 1)
    half = buckets // 2
    exact = half // 2
    side = np.where(offsets > 0, half, 0)
    distance = np.abs(offsets)
    safe = np.maximum(distance, 1)
    large = exact + (np.log(safe / exact) / np.log(reach / exact) * (half - exact)).astype(np.int64)
    large = np.minimum(large, half - 1)
    return side + np.where(distance < exact, distance, large)


def magnitude_steps(span, reach):
    half = BUCKETS // 2
    exact = half // 2
    offsets = np.arange(span + 1)
    table = bucket_table(span, BUCKETS, reach)[span:]
    magnitude = table - np.where(offsets > 0, half, 0)
    steps = []
    for level in range(exact + 1, half):
        if (magnitude >= level).any():
            steps.append(int(np.argmax(magnitude >= level)))
    return steps


def bucket_index(offset, span, reach):
    half = BUCKETS // 2
    exact = half // 2
    distance = jnp.abs(offset)
    magnitude = jnp.minimum(distance, exact)
    for edge in magnitude_steps(span, reach):
        magnitude = magnitude + (distance >= edge).astype(jnp.int32)
    return magnitude + jnp.where(offset > 0, half, 0)


def rel_marks(slots, zero):
    places = np.arange(slots)
    offset = np.where(places < 768, places - zero, -300)
    table = bucket_table(slots - 1, BUCKETS, token_reach)
    return table[offset + slots - 1][None, :] == np.arange(BUCKETS)[:, None]


def write_marks(marks_ref, x_tile, y_tile, begin=0):
    one = jnp.ones(x_tile.shape, jnp.bfloat16)
    zero = jnp.zeros(x_tile.shape, jnp.bfloat16)
    cols = slice(begin, begin + x_tile.shape[1])
    for b in range(BUCKETS):
        marks_ref[b * 16 : b * 16 + 16, cols] = jnp.where(x_tile == b, one, zero)
        marks_ref[512 + b * 16 : 512 + b * 16 + 16, cols] = jnp.where(y_tile == b, one, zero)


def index_kernel(len_ref, box_ref, turned_ref, ix_ref, iy_ref):
    place = lax.broadcasted_iota(jnp.int32, ix_ref.shape, 1)
    x_bucket = bucket_index(box_ref[0:1, :] - turned_ref[:, 0:1], coord_top, layout_reach)
    y_bucket = bucket_index(box_ref[1:2, :] - turned_ref[:, 1:2], coord_top, layout_reach)
    x_bucket = jnp.where(place < len_ref[0], x_bucket, DEAD_BUCKET)
    ix_ref[...] = x_bucket.astype(jnp.float32).astype(jnp.bfloat16)
    iy_ref[...] = y_bucket.astype(jnp.float32).astype(jnp.bfloat16)


def index_call(length, box):
    slots = box.shape[1]
    tile = pl.BlockSpec((BIAS_TILE, slots), lambda i: (i, 0))
    return pl.pallas_call(
        index_kernel,
        grid=(slots // BIAS_TILE,),
        in_specs=[
            pl.BlockSpec(memory_space=pltpu.SMEM),
            pl.BlockSpec((2, slots), lambda i: (0, 0)),
            pl.BlockSpec((BIAS_TILE, 2), lambda i: (i, 0)),
        ],
        out_specs=[tile, tile],
        out_shape=[jax.ShapeDtypeStruct((slots, slots), jnp.bfloat16)] * 2,
        name="index",
        **params_for(1e9, 4e6),
    )(length, box, box.T)


def prepare_kernel(tables_ref, marks_ref, lhs_ref, skew_ref):
    slots = marks_ref.shape[1]
    tables = tables_ref[...]
    rel_row = jnp.dot(
        tables[:, :BUCKETS], marks_ref[...], preferred_element_type=jnp.float32
    )
    for h in range(HEADS):
        wide = jnp.broadcast_to(rel_row[h : h + 1, :], (BIAS_TILE, slots))
        skew = pltpu.roll(wide, 0, 1, stride=1, stride_axis=0)[:, :640]
        skew_ref[h] = skew.astype(jnp.bfloat16)
    tall, long = HEADS * 16, 2 * BUCKETS * 16
    layout = tables[:, BUCKETS:]
    dead = lax.broadcasted_iota(jnp.int32, layout.shape, 1) == DEAD_BUCKET
    layout = jnp.where(dead, jnp.asarray(masked_score, jnp.bfloat16), layout)
    head_of = lax.broadcasted_iota(jnp.int32, (tall, HEADS), 0) // 16
    pick_head = head_of == lax.broadcasted_iota(jnp.int32, (tall, HEADS), 1)
    bucket_of = lax.broadcasted_iota(jnp.int32, (2 * BUCKETS, long), 1) // 16
    pick_bucket = bucket_of == lax.broadcasted_iota(jnp.int32, (2 * BUCKETS, long), 0)
    by_head = jnp.dot(
        pick_head.astype(jnp.bfloat16), layout, preferred_element_type=jnp.float32
    ).astype(jnp.bfloat16)
    full = jnp.dot(
        by_head, pick_bucket.astype(jnp.bfloat16), preferred_element_type=jnp.float32
    )
    same = (
        lax.broadcasted_iota(jnp.int32, (tall, long), 0) % 16
        == lax.broadcasted_iota(jnp.int32, (tall, long), 1) % 16
    )
    lhs_ref[...] = jnp.where(same, full, 0.0).astype(jnp.bfloat16)


def prepare_call(tables, slots):
    return pl.pallas_call(
        prepare_kernel,
        out_shape=[
            jax.ShapeDtypeStruct((HEADS * 16, 2 * BUCKETS * 16), jnp.bfloat16),
            jax.ShapeDtypeStruct((HEADS, BIAS_TILE, 640), jnp.bfloat16),
        ],
        name="prepare",
        **params_for(1e9, 6e6),
    )(tables, jnp.asarray(rel_marks(slots, 256)).astype(jnp.bfloat16))


def two_at_a_time(ix_ref, iy_ref, first_ref, second_ref, use, joint=1):
    rows, slots = ix_ref.shape
    step = 16 * joint

    def write(ref, r0):
        for at in range(joint):
            here = pl.multiple_of(jnp.minimum(r0 + 16 * at, rows - 16), 16)
            write_marks(ref, ix_ref[pl.ds(here, 16), :], iy_ref[pl.ds(here, 16), :], at * slots)

    write(first_ref, 0)

    def body(t, carry):
        r0 = pl.multiple_of(t * 2 * step, 2 * step)
        write(second_ref, r0 + step)
        use(r0, first_ref)
        write(first_ref, r0 + 2 * step)
        use(pl.multiple_of(r0 + step, step), second_ref)
        return carry

    lax.fori_loop(0, rows // (2 * step), body, 0)


def bias_kernel(first, ix_ref, iy_ref, lhs_ref, skew_ref, *rest):
    bias_ref, first_ref, second_ref = rest[-3:]
    block = pl.program_id(0) + first
    slots = ix_ref.shape[1]

    def use(r0, marks_ref):
        out = jnp.dot(lhs_ref[...], marks_ref[...], preferred_element_type=jnp.float32)
        for c in range(slots // 128):
            shift = pl.multiple_of((jnp.clip(c - block, -2, 2) + 2) * 128, 128)
            cols = slice(c * 128, c * 128 + 128)
            for h in range(HEADS):
                bias_ref[h, pl.ds(r0, 16), cols] = out[
                    h * 16 : h * 16 + 16, cols
                ] + skew_ref[h, pl.ds(r0, 16), pl.ds(shift, 128)].astype(jnp.float32)

    two_at_a_time(ix_ref, iy_ref, first_ref, second_ref, use)


def bias_call(ix, iy, lhs, skew, begin, end, held=None):
    slots = ix.shape[0]
    tile = pl.BlockSpec((BIAS_TILE, slots), lambda i: (i + begin, 0))
    in_specs = [
        tile,
        tile,
        pl.BlockSpec(lhs.shape, lambda i: (0, 0)),
        pl.BlockSpec(skew.shape, lambda i: (0, 0, 0)),
    ]
    args = [ix, iy, lhs, skew]
    aliases = {}
    if held is not None:
        in_specs.append(pl.BlockSpec(memory_space=pl.ANY))
        args.append(held)
        aliases = {4: 0}
    share = (end - begin) * BIAS_TILE / slots
    return pl.pallas_call(
        functools.partial(bias_kernel, begin),
        grid=(end - begin,),
        in_specs=in_specs,
        out_specs=pl.BlockSpec((HEADS, BIAS_TILE, slots), lambda i: (0, i + begin, 0)),
        out_shape=jax.ShapeDtypeStruct((HEADS, slots, slots), jnp.float32),
        scratch_shapes=[pltpu.VMEM((2 * BUCKETS * 16, slots), jnp.bfloat16)] * 2,
        input_output_aliases=aliases,
        name="bias",
        **params_for(34e9 * share, 72e6 * share),
    )(*args)


def own_lanes(h):
    left = lax.broadcasted_iota(jnp.int32, (1, 128), 1) < HEAD_DIM
    return left if h == 0 else jnp.logical_not(left)


def attend_kernel(q_ref, k_ref, v_ref, bias_ref, probs_ref, mixed_ref):
    q, k, v = q_ref[...], k_ref[...], v_ref[...]
    outs = []
    for h in range(2):
        q_own = jnp.where(own_lanes(h), q, jnp.zeros_like(q))
        scores = lax.dot_general(
            q_own, k, (((1,), (1,)), ((), ())), preferred_element_type=jnp.float32
        )
        strips = []
        for r in range(0, q.shape[0], STRIP):
            strip = scores[r : r + STRIP] + bias_ref[h, r : r + STRIP, :]
            top = jnp.max(strip, axis=1, keepdims=True)
            weights = jnp.exp(strip - top)
            total = jnp.sum(weights, axis=1, keepdims=True)
            strips.append((weights * (1.0 / total)).astype(jnp.bfloat16))
        probs = jnp.concatenate(strips, axis=0)
        probs_ref[h] = probs
        outs.append(jnp.dot(probs, v, preferred_element_type=jnp.float32))
    mixed_ref[...] = jnp.where(own_lanes(0), outs[0], outs[1]).astype(jnp.bfloat16)


def attend_call(query, key_rows, value_rows, bias):
    slots, inner = query.shape
    pairs = inner // 128
    tile = min(ROW_TILE, slots)
    rows = pl.BlockSpec((tile, 128), lambda p, i: (i, p))
    square = pl.BlockSpec((2, tile, slots), lambda p, i: (p, i, 0))
    return pl.pallas_call(
        attend_kernel,
        grid=(pairs, slots // tile),
        in_specs=[
            rows,
            pl.BlockSpec((slots, 128), lambda p, i: (0, p)),
            pl.BlockSpec((slots, 128), lambda p, i: (0, p)),
            square,
        ],
        out_specs=[square, rows],
        out_shape=[
            jax.ShapeDtypeStruct((HEADS, slots, slots), jnp.bfloat16),
            jax.ShapeDtypeStruct((slots, inner), jnp.bfloat16),
        ],
        name="attend",
        **params_for(34e9, 100e6),
    )(query, key_rows, value_rows, bias)


def attend_back_kernel(q_ref, k_ref, v_ref, grad_ref, probs_ref, *rest):
    ds_ref, dq_ref, dk_ref, dv_ref, k_sum, v_sum = rest[-6:]
    step = pl.program_id(1)
    q, k, v, grad = q_ref[...], k_ref[...], v_ref[...], grad_ref[...]
    q_turned, grad_turned = q.T, grad.T

    @pl.when(step == 0)
    def _():
        k_sum[...] = jnp.zeros_like(k_sum)
        v_sum[...] = jnp.zeros_like(v_sum)

    outs = []
    for h in range(2):
        grad_own = jnp.where(own_lanes(h), grad, jnp.zeros_like(grad))
        grad_probs = lax.dot_general(
            grad_own, v, (((1,), (1,)), ((), ())), preferred_element_type=jnp.float32
        )
        strips = []
        for r in range(0, q.shape[0], STRIP):
            probs = probs_ref[h, r : r + STRIP, :].astype(jnp.float32)
            terms = probs * grad_probs[r : r + STRIP]
            delta = jnp.sum(terms, axis=1, keepdims=True)
            strips.append((terms - probs * delta).astype(jnp.bfloat16))
        ds = jnp.concatenate(strips, axis=0)
        ds_ref[h] = ds
        outs.append(jnp.dot(ds, k, preferred_element_type=jnp.float32))
        own = slice(h * HEAD_DIM, (h + 1) * HEAD_DIM)
        k_sum[own, :] += jnp.dot(q_turned[own], ds, preferred_element_type=jnp.float32)
        v_sum[own, :] += jnp.dot(
            grad_turned[own], probs_ref[h], preferred_element_type=jnp.float32
        )
    dq_ref[...] = jnp.where(own_lanes(0), outs[0], outs[1]).astype(jnp.bfloat16)

    @pl.when(step == pl.num_programs(1) - 1)
    def _():
        dk_ref[...] = k_sum[...].T.astype(jnp.bfloat16)
        dv_ref[...] = v_sum[...].T.astype(jnp.bfloat16)


def attend_back_call(query, key_rows, value_rows, grad_mixed, probs, begin, end, held=None):
    slots, inner = query.shape
    tile = min(ROW_TILE, slots)
    rows = pl.BlockSpec((tile, 128), lambda p, i: (i, p + begin))
    whole = pl.BlockSpec((slots, 128), lambda p, i: (0, p + begin))
    square = pl.BlockSpec((2, tile, slots), lambda p, i: (p + begin, i, 0))
    args = [query, key_rows, value_rows, grad_mixed, probs]
    in_specs = [rows, whole, whole, rows, square]
    aliases = {}
    if held is not None:
        aliases = {len(args) + at: at for at in range(len(held))}
        in_specs += [pl.BlockSpec(memory_space=pl.ANY)] * len(held)
        args += list(held)
    share = (end - begin) * 128 / inner
    return pl.pallas_call(
        attend_back_kernel,
        grid=(end - begin, slots // tile),
        in_specs=in_specs,
        out_specs=[square, rows, whole, whole],
        out_shape=[jax.ShapeDtypeStruct((HEADS, slots, slots), jnp.bfloat16)]
        + [jax.ShapeDtypeStruct((slots, inner), jnp.bfloat16)] * 3,
        scratch_shapes=[pltpu.VMEM((128, slots), jnp.float32)] * 2,
        input_output_aliases=aliases,
        name="attend_back",
        **params_for(34e9 * share, 72e6 * share),
    )(*args)


def rel_near_marks(slots):
    row = np.arange(BIAS_TILE)[:, None]
    offset = np.arange(640)[None, :] - 256 - row
    bucket = bucket_table(slots - 1, BUCKETS, token_reach)[offset + slots - 1]
    marks = bucket[None, :, :] == np.arange(BUCKETS)[:, None, None]
    marks = marks.reshape(BUCKETS, BIAS_TILE // 16, 16, 640).transpose(1, 0, 2, 3)
    return marks.reshape(BIAS_TILE // 16, BUCKETS * 16, 640)


def table_kernel(
    first, ds_ref, ix_ref, iy_ref, near_ref, out_ref, total, rel_total, first_ref, second_ref
):
    step = pl.program_id(0)
    block = step + first
    slots = ix_ref.shape[1]
    blocks = slots // BIAS_TILE
    heads = ds_ref.shape[0]

    @pl.when(step == 0)
    def _():
        total[...] = jnp.zeros_like(total)
        rel_total[...] = jnp.zeros_like(rel_total)

    begin = jnp.clip(block - 1, 0, blocks - 3)
    lanes = pl.ds(pl.multiple_of(begin * BIAS_TILE, BIAS_TILE), 3 * BIAS_TILE)
    source = pl.ds(
        pl.multiple_of((begin - block + 2) * BIAS_TILE, BIAS_TILE), 3 * BIAS_TILE
    )
    place = lax.broadcasted_iota(jnp.int32, (16, TABLE_JOINT * slots), 1) % slots
    low = (place < begin * BIAS_TILE).astype(jnp.float32).astype(jnp.bfloat16)
    high = (place >= (begin + 3) * BIAS_TILE).astype(jnp.float32).astype(jnp.bfloat16)
    for ref in (first_ref, second_ref):
        ref[2 * BUCKETS * 16 : 2 * BUCKETS * 16 + 16, :] = low
        ref[2 * BUCKETS * 16 + 16 :, :] = high

    def use(r0, marks_ref):
        ds, close, near = [], [], []
        for at in range(TABLE_JOINT):
            here = pl.ds(pl.multiple_of(r0 + 16 * at, 16), 16)
            ds.append(ds_ref[:, here, :].reshape(heads * 16, slots))
            close.append(ds_ref[:, here, lanes].reshape(heads * 16, 3 * BIAS_TILE))
            near.append(near_ref[r0 // 16 + at, :, source])
        total[...] += right_transposed(marks_ref[...], jnp.concatenate(ds, axis=1))
        rel_total[...] += right_transposed(
            jnp.concatenate(near, axis=1), jnp.concatenate(close, axis=1)
        )

    two_at_a_time(ix_ref, iy_ref, first_ref, second_ref, use, TABLE_JOINT)

    @pl.when(step == pl.num_programs(0) - 1)
    def _():
        at = 0
        for ref in (total, rel_total):
            shape = ref.shape
            same = (
                lax.broadcasted_iota(jnp.int32, shape, 0) % 16
                == lax.broadcasted_iota(jnp.int32, shape, 1) % 16
            )
            kept = jnp.where(same, ref[...], 0.0).reshape(shape[0] // 16, 16, shape[1])
            out_ref[at : at + shape[0] // 16, :] = kept.sum(axis=1)
            at += shape[0] // 16
        out_ref[at:, :] = jnp.zeros((out_ref.shape[0] - at, out_ref.shape[1]), jnp.float32)


def table_call(ds, ix, iy, begin, end):
    slots = ix.shape[0]
    tile = pl.BlockSpec((BIAS_TILE, slots), lambda i: (i + begin, 0))
    share = (end - begin) * BIAS_TILE / slots
    near = jnp.asarray(rel_near_marks(slots)).astype(jnp.bfloat16)
    marked = (2 * BUCKETS + 2) * 16
    return pl.pallas_call(
        functools.partial(table_kernel, begin),
        grid=(end - begin,),
        in_specs=[
            pl.BlockSpec((HEADS, BIAS_TILE, slots), lambda i: (0, i + begin, 0)),
            tile,
            tile,
            pl.BlockSpec(near.shape, lambda i: (0, 0, 0)),
        ],
        out_specs=pl.BlockSpec((104, HEADS * 16), lambda i: (0, 0)),
        out_shape=jax.ShapeDtypeStruct((104, HEADS * 16), jnp.float32),
        scratch_shapes=[
            pltpu.VMEM((marked, HEADS * 16), jnp.float32),
            pltpu.VMEM((BUCKETS * 16, HEADS * 16), jnp.float32),
            pltpu.VMEM((marked, TABLE_JOINT * slots), jnp.bfloat16),
            pltpu.VMEM((marked, TABLE_JOINT * slots), jnp.bfloat16),
        ],
        name="table_back",
        **params_for(40e9 * share, 40e6 * share),
    )(ds, ix, iy, near)


def table_finish(parts):
    sums = sum(parts).reshape(104, HEADS, 16).sum(axis=2).T
    near = sums[:, 66:98]
    left, right = BUCKETS // 2 - 1, BUCKETS - 1
    column = jnp.arange(BUCKETS)[None, :]
    rel = near + jnp.where(column == left, sums[:, 64:65], 0.0)
    rel = rel + jnp.where(column == right, sums[:, 65:66], 0.0)
    return rel, sums[:, :BUCKETS], sums[:, BUCKETS : 2 * BUCKETS]


def ffn_kernel(
    unit, core_ref, n_ref, seed_ref, hidden_ref, gate_ref, up_ref, down_ref,
    out_ref, dn_ref, gate_away_ref, gate_stay_ref, up_away_ref, up_stay_ref, ddown_ref,
    out_sum, turned_ref,
):
    step = pl.program_id(0)
    width = n_ref.shape[1]
    half = width // 2

    @pl.when(step == 0)
    def _():
        out_sum[...] = hidden_ref[...]
        dn_ref[...] = jnp.zeros_like(dn_ref)
        core = core_ref[0]
        for lanes in range(0, width, 128):
            turned = n_ref[:, lanes : lanes + 128].T
            for part in range(128 // unit):
                group = lanes // unit + part
                first = jnp.where(core == group % 2, half, 0) + group // 2 * unit
                turned_ref[pl.ds(pl.multiple_of(first, 16), unit), :] = turned[
                    part * unit : (part + 1) * unit
                ]

    seed = seed_ref[...]
    w_gate, w_up, w_down = gate_ref[...], up_ref[...], down_ref[...]
    gate = plain_product(n_ref[...], w_gate)
    upper = plain_product(n_ref[...], w_up)
    grad_act = right_transposed(seed, w_down)
    square = gate * gate
    tanh = jnp.tanh(gelu_scale * (gate + 0.044715 * gate * square))
    cdf = 0.5 * (1.0 + tanh)
    gelu = gate * cdf
    slope = cdf + 0.5 * gate * (1.0 - tanh * tanh) * gelu_scale * (1.0 + 3 * 0.044715 * square)
    activated = (gelu * upper).astype(jnp.bfloat16)
    grad_gate = (grad_act * upper * slope).astype(jnp.bfloat16)
    grad_upper = (grad_act * gelu).astype(jnp.bfloat16)
    out_sum[...] += plain_product(activated, w_down)
    dn_ref[...] += right_transposed(grad_gate, w_gate) + right_transposed(grad_upper, w_up)
    d_gate = plain_product(turned_ref[...], grad_gate).astype(jnp.bfloat16)
    gate_away_ref[...] = d_gate[:half]
    gate_stay_ref[...] = d_gate[half:]
    d_up = plain_product(turned_ref[...], grad_upper).astype(jnp.bfloat16)
    up_away_ref[...] = d_up[:half]
    up_stay_ref[...] = d_up[half:]
    ddown_ref[...] = left_transposed(activated, seed).astype(jnp.bfloat16)

    @pl.when(step == pl.num_programs(0) - 1)
    def _():
        out_ref[...] = out_sum[...].astype(jnp.bfloat16)


def ffn_call(core, unit, normed, seed, hidden, packed, w_down):
    slots, width = normed.shape
    ff = w_down.shape[0]
    tile = 256
    count = ff // tile
    full = pl.BlockSpec((slots, width), lambda f: (0, 0))
    column = pl.BlockSpec((width // 2, tile), lambda f: (0, f))
    row = pl.BlockSpec((tile, width), lambda f: (f, 0))
    return pl.pallas_call(
        functools.partial(ffn_kernel, unit),
        grid=(count,),
        in_specs=[
            pl.BlockSpec(memory_space=pltpu.SMEM),
            full,
            full,
            full,
            pl.BlockSpec((width, tile), lambda f: (0, f)),
            pl.BlockSpec((width, tile), lambda f: (0, f + count)),
            row,
        ],
        out_specs=[full, full, column, column, column, column, row],
        out_shape=[
            jax.ShapeDtypeStruct((slots, width), jnp.bfloat16),
            jax.ShapeDtypeStruct((slots, width), jnp.float32),
        ]
        + [jax.ShapeDtypeStruct((width // 2, ff), jnp.bfloat16)] * 4
        + [jax.ShapeDtypeStruct((ff, width), jnp.bfloat16)],
        scratch_shapes=[
            pltpu.VMEM((slots, width), jnp.float32),
            pltpu.VMEM((width, slots), jnp.bfloat16),
        ],
        name="ffn",
        **params_for(18 * slots * width * ff, 50e6),
    )(core, normed, seed, hidden, packed, packed, w_down)


class Exchange:
    def __init__(self, mesh):
        self.count = mesh.shape["wide"] * mesh.shape["narrow"]
        self.bits = self.count.bit_length() - 1
        assert self.count == 1 << self.bits
        one, two, three, *tail = [b for b in range(self.bits) if b != CORE_BIT]
        self.orders = (
            [CORE_BIT, one, two] + tail + [three],
            [CORE_BIT, two, three, one] + tail,
            [CORE_BIT, three, one, two] + tail,
        )

    def me(self):
        return lax.axis_index(AXES)

    def mine(self, bit):
        return (self.me() >> bit) & 1

    def swap(self, value, bit):
        pairs = [(d, d ^ (1 << bit)) for d in range(self.count)]
        return lax.ppermute(value, AXES, pairs)

    def spread(self, shard):
        copies = jnp.broadcast_to(shard[None, :], (self.count, shard.shape[0]))
        return lax.all_to_all(copies, AXES, 0, 0, tiled=True)

    def sum_small(self, terms):
        return jnp.sum(lax.all_to_all(terms, AXES, 0, 0, tiled=True), axis=0)


class Gather:
    def __init__(self, exchange, shard, order):
        self.exchange = exchange
        self.value = shard[None]
        self.steps = list(reversed(exchange.orders[order]))
        self.offsets = [0]
        self.flight = None

    def done(self):
        return not self.steps

    def go(self):
        self.flight = self.exchange.swap(self.value, self.steps[0])

    def land(self):
        bit = self.steps.pop(0)
        other, self.flight = self.flight, None
        self.offsets += [offset | 1 << bit for offset in self.offsets]
        if self.steps:
            self.value = jnp.concatenate([self.value, other], axis=0)
        else:
            self.other = other


def project_kernel(offsets, me_ref, x_ref, *refs):
    count = len(offsets)
    halves, outs, scratch = refs[: 2 * count], refs[2 * count : 4 * count], refs[4 * count]
    me = me_ref[0]
    for at in range(count):
        value_ref, other_ref = halves[2 * at : 2 * at + 2]
        out_ref, full_ref = outs[2 * at : 2 * at + 2]
        places, rows, _ = value_ref.shape
        for place, offset in enumerate(offsets[at]):
            part = value_ref[place] if place < places else other_ref[place - places]
            begin = pl.multiple_of((me ^ offset) * rows, rows)
            scratch[at, pl.ds(begin, rows), :] = part
        full_ref[...] = scratch[at]
        out_ref[...] = plain_product(x_ref[...], scratch[at]).astype(jnp.bfloat16)


def project_call(exchange, normed, tasks):
    places, rows, inner = tasks[0].value.shape
    slots, width = normed.shape
    if rows % 16:
        fulls, outs = [], []
        for task in tasks:
            held = jnp.concatenate([task.value, task.other], axis=0)
            place_of = np.argsort(np.asarray(task.offsets))
            spots = jnp.asarray(place_of)[exchange.me() ^ jnp.arange(exchange.count)]
            fulls.append(jnp.take(held, spots, axis=0).reshape(width, inner))
            outs.append(plain_product(normed, fulls[-1]).astype(jnp.bfloat16))
        return outs, fulls
    tile = 256
    part = pl.BlockSpec((places, rows, tile), lambda n: (0, 0, n))
    column = pl.BlockSpec((slots, tile), lambda n: (0, n))
    full = pl.BlockSpec((width, tile), lambda n: (0, n))
    results = pl.pallas_call(
        functools.partial(project_kernel, tuple(tuple(task.offsets) for task in tasks)),
        grid=(inner // tile,),
        in_specs=[
            pl.BlockSpec(memory_space=pltpu.SMEM),
            pl.BlockSpec((slots, width), lambda n: (0, 0)),
        ]
        + [part] * (2 * len(tasks)),
        out_specs=[column, full] * len(tasks),
        out_shape=[
            jax.ShapeDtypeStruct((slots, inner), jnp.bfloat16),
            jax.ShapeDtypeStruct((width, inner), jnp.bfloat16),
        ]
        * len(tasks),
        scratch_shapes=[pltpu.VMEM((len(tasks), width, tile), jnp.bfloat16)],
        name="project",
        **params_for(2 * len(tasks) * slots * width * inner, 20e6),
    )(
        exchange.me().astype(jnp.int32).reshape(1),
        normed,
        *[half for task in tasks for half in (task.value, task.other)],
    )
    return results[0::2], results[1::2]


class Scatter:
    def __init__(self, exchange, terms, order, away=None):
        self.exchange = exchange
        self.held = list(range(exchange.bits - 1, -1, -1))
        if away is not None:
            self.held.remove(CORE_BIT)
        dims = (2,) * len(self.held)
        rows = terms.shape[0] >> len(self.held)
        self.value = terms.reshape(dims + (rows,) + terms.shape[1:])
        self.away = None if away is None else away.reshape(self.value.shape)
        self.steps = list(exchange.orders[order])
        self.flight = None

    def done(self):
        return not self.steps

    def go(self):
        bit = self.steps[0]
        if self.away is not None:
            self.flight = self.exchange.swap(self.away, bit)
            return
        self.spot = self.held.index(bit)
        away = lax.dynamic_index_in_dim(
            self.value, 1 - self.exchange.mine(bit), self.spot, keepdims=False
        )
        self.flight = self.exchange.swap(away, bit)

    def land(self):
        bit = self.steps.pop(0)
        other, self.flight = self.flight, None
        stay = self.value
        if self.away is None:
            stay = lax.dynamic_index_in_dim(
                self.value, self.exchange.mine(bit), self.spot, keepdims=False
            )
            self.held.pop(self.spot)
        self.away = None
        value = stay.astype(jnp.float32) + other.astype(jnp.float32)
        if self.steps:
            value = value.astype(jnp.bfloat16)
        self.value = value


class Traffic:
    limit = 5

    def __init__(self):
        self.tasks = []

    def add(self, *tasks):
        self.tasks += tasks
        self.send()

    def send(self):
        busy = sum(task.flight is not None for task in self.tasks)
        for task in self.tasks:
            if task.flight is None and busy < self.limit:
                task.go()
                busy += 1

    def step(self, *work):
        flying = [task for task in self.tasks if task.flight is not None]
        work, flights = lax.optimization_barrier((work, [task.flight for task in flying]))
        for task, flight in zip(flying, flights):
            task.flight = flight
            task.land()
        self.tasks = [task for task in self.tasks if not task.done()]
        self.send()
        return work[0] if len(work) == 1 else work


def norm_apply(values, gain):
    return values * lax.rsqrt(jnp.mean(values * values, axis=-1, keepdims=True) + epsilon) * gain


def layer(
    exchange, inputs, norm_first, w_query, w_key, w_value, w_out, rel_table, x_table, y_table,
    norm_second, w_gate, w_up, w_down, lengths, boxes, cotangent,
):
    seq_count, slots, width = inputs.shape
    inner = w_query.shape[1]
    count = exchange.count
    entries = rel_table.shape[0]
    span = norm_first.shape[0]

    rows = inputs.reshape(slots, width).astype(jnp.float32)
    seed = cotangent.reshape(slots, width)
    traffic = Traffic()
    qkv_tasks = [
        Gather(exchange, shard, order) for order, shard in enumerate((w_query, w_key, w_value))
    ]
    traffic.add(*qkv_tasks)
    small = exchange.spread(
        jnp.concatenate([norm_first, norm_second, rel_table, x_table, y_table])
    )
    packed = lax.all_gather(
        jnp.concatenate([w_gate, w_up, w_out], axis=1), AXES, axis=0, tiled=True
    )
    down_full = lax.all_gather(w_down, AXES, axis=0, tiled=True)
    ix, iy = index_call(lengths, boxes[0])
    gain_one = small[:, :span].reshape(-1).astype(jnp.float32)
    gain_two = small[:, span : 2 * span].reshape(-1).astype(jnp.float32)
    tables = jnp.concatenate(
        [
            small[:, 2 * span + at * entries : 2 * span + (at + 1) * entries].reshape(
                HEADS, BUCKETS
            )
            for at in range(3)
        ],
        axis=1,
    )
    lhs, skew = prepare_call(tables, slots)
    blocks = slots // BIAS_TILE
    pieces = exchange.bits - 1
    bias = None
    for piece in range(pieces):
        begin, end = piece * blocks // pieces, (piece + 1) * blocks // pieces
        if bias is None:
            lhs = traffic.step(lhs)
        else:
            lhs, bias = traffic.step(lhs, bias)
        if end > begin:
            bias = bias_call(ix, iy, lhs, skew, begin, end, bias)
    normed_one = norm_apply(rows, gain_one).astype(jnp.bfloat16)
    normed_one, bias = traffic.step(normed_one, bias)
    projected, fulls = project_call(exchange, normed_one, qkv_tasks)
    query, key_rows, value_rows = projected
    query_full, key_full, value_full = fulls
    probs, mixed = attend_call(query, key_rows, value_rows, bias)
    out_full = packed[:, 2 * w_gate.shape[1] :]
    hidden = rows + plain_product(mixed, out_full)
    normed_two = norm_apply(hidden, gain_two).astype(jnp.bfloat16)
    core = exchange.mine(CORE_BIT).astype(jnp.int32).reshape(1)
    unit = width // count << CORE_BIT
    output, grad_normed_two, gate_away, gate_stay, up_away, up_stay, d_down = ffn_call(
        core, unit, normed_two, seed, hidden, packed, down_full
    )
    ffn_tasks = [
        Scatter(exchange, gate_stay, 0, gate_away),
        Scatter(exchange, up_stay, 1, up_away),
        Scatter(exchange, d_down, 2),
    ]
    traffic.add(*ffn_tasks)
    unused_two, norm_two_pull = jax.vjp(norm_apply, hidden, gain_two)
    hidden_part, grad_gain_two = norm_two_pull(grad_normed_two)
    grad_hidden = seed.astype(jnp.float32) + hidden_part
    branch_low = grad_hidden.astype(jnp.bfloat16)
    d_out = left_transposed(mixed, branch_low).astype(jnp.bfloat16)
    grad_mixed = right_transposed(branch_low, out_full).astype(jnp.bfloat16)
    grad_mixed, d_out = traffic.step(grad_mixed, d_out)
    out_task = Scatter(exchange, d_out, 0)
    traffic.add(out_task)
    pairs = inner // 128
    cuts = (0, 3 * pairs // 8, 6 * pairs // 8, pairs)
    back = None
    for begin, end in zip(cuts[:-1], cuts[1:]):
        back = attend_back_call(
            query, key_rows, value_rows, grad_mixed, probs, begin, end, back
        )
        back = traffic.step(back)
    ds, dq, dk, dv = back
    d_weights = [left_transposed(normed_one, part).astype(jnp.bfloat16) for part in (dq, dk, dv)]
    dq, d_weights = traffic.step(dq, d_weights)
    w_tasks = [Scatter(exchange, part, at) for at, part in enumerate(d_weights)]
    traffic.add(*w_tasks)
    grad_normed_one = (
        right_transposed(dq, query_full)
        + right_transposed(dk, key_full)
        + right_transposed(dv, value_full)
    )
    grad_normed_one, ix = traffic.step(grad_normed_one, ix)
    unused_one, norm_one_pull = jax.vjp(norm_apply, rows, gain_one)
    rows_part, grad_gain_one = norm_one_pull(grad_normed_one)
    grad_inputs = (grad_hidden + rows_part).reshape(inputs.shape)
    parts = []
    pieces = 4
    for piece in range(pieces):
        begin, end = piece * blocks // pieces, (piece + 1) * blocks // pieces
        parts.append(table_call(ds, ix, iy, begin, end))
        if piece + 1 < pieces:
            ix, parts = traffic.step(ix, parts)
    grad_rel, grad_x, grad_y = table_finish(parts)
    g_small = exchange.sum_small(
        jnp.concatenate(
            [
                part.reshape(count, -1)
                for part in (grad_gain_one, grad_gain_two, grad_rel, grad_x, grad_y)
            ],
            axis=1,
        )
    )
    while traffic.tasks:
        g_small = traffic.step(g_small)
    g_gate, g_up, g_down = (task.value for task in ffn_tasks)
    edges = [0, span, 2 * span, 2 * span + entries, 2 * span + 2 * entries, g_small.shape[0]]
    g_small = [g_small[a:b] for a, b in zip(edges[:-1], edges[1:])]
    return (
        output.reshape(inputs.shape),
        grad_inputs,
        g_small[0],
        w_tasks[0].value,
        w_tasks[1].value,
        w_tasks[2].value,
        out_task.value,
        g_small[2],
        g_small[3],
        g_small[4],
        g_small[1],
        g_gate,
        g_up,
        g_down,
    )


def solution(mesh):
    exchange = Exchange(mesh)
    vector, matrix, cube = P(AXES), P(AXES, None), P(AXES, None, None)
    in_specs = (
        (cube, vector)
        + (matrix,) * 4
        + (vector,) * 4
        + (matrix,) * 3
        + (vector, cube, cube)
    )
    out_specs = (cube, cube, vector) + (matrix,) * 4 + (vector,) * 4 + (matrix,) * 3

    def local(*args):
        return layer(exchange, *args)

    return jax.shard_map(local, mesh=mesh, in_specs=in_specs, out_specs=out_specs, check_vma=False)
```

```python
import functools

import jax
import jax.numpy as jnp
import numpy as np
from jax import lax
from jax.experimental import pallas as pl
from jax.experimental.pallas import tpu as pltpu
from jax.sharding import PartitionSpec as P

HEADS = 16
HEAD_DIM = 64
BUCKETS = 32
AXES = ("wide", "narrow")

epsilon = 1e-06
coord_top = 1000
token_reach = 128
layout_reach = 256
masked_score = -1e30
gelu_scale = 0.7978845608028654

VMEM_LIMIT = 60 * 2**20
ROW_TILE = 1024
STRIP = 16
BIAS_TILE = 128
DEAD_BUCKET = 16
CORE_BIT = 1
TABLE_JOINT = 4


def params_for(flops, moved):
    return dict(
        compiler_params=pltpu.CompilerParams(vmem_limit_bytes=VMEM_LIMIT),
        cost_estimate=pl.CostEstimate(
            flops=int(flops), bytes_accessed=int(moved), transcendentals=0
        ),
    )


def plain_product(left, right):
    return jnp.dot(left, right, preferred_element_type=jnp.float32)


def left_transposed(left, right):
    return lax.dot_general(
        left, right, (((0,), (0,)), ((), ())), preferred_element_type=jnp.float32
    )


def right_transposed(left, right):
    return lax.dot_general(
        left, right, (((1,), (1,)), ((), ())), preferred_element_type=jnp.float32
    )


def bucket_table(span, buckets, reach):
    offsets = np.arange(-span, span + 1)
    half = buckets // 2
    exact = half // 2
    side = np.where(offsets > 0, half, 0)
    distance = np.abs(offsets)
    safe = np.maximum(distance, 1)
    large = exact + (np.log(safe / exact) / np.log(reach / exact) * (half - exact)).astype(np.int64)
    large = np.minimum(large, half - 1)
    return side + np.where(distance < exact, distance, large)


def magnitude_steps(span, reach):
    half = BUCKETS // 2
    exact = half // 2
    offsets = np.arange(span + 1)
    table = bucket_table(span, BUCKETS, reach)[span:]
    magnitude = table - np.where(offsets > 0, half, 0)
    steps = []
    for level in range(exact + 1, half):
        if (magnitude >= level).any():
            steps.append(int(np.argmax(magnitude >= level)))
    return steps


def bucket_index(offset, span, reach):
    half = BUCKETS // 2
    exact = half // 2
    distance = jnp.abs(offset)
    edges = magnitude_steps(span, reach)
    edges = [exact] + edges + [2 * span] * (exact - 1 - len(edges))

    def search(low, high):
        if high - low == 1:
            return low
        middle = (low + high) // 2
        return jnp.where(distance >= edges[middle], search(middle, high), search(low, middle))

    magnitude = jnp.where(distance < exact, distance, exact + search(0, len(edges)))
    return magnitude + jnp.where(offset > 0, half, 0)


def rel_marks(slots, zero):
    places = np.arange(slots)
    offset = np.where(places < 768, places - zero, -300)
    table = bucket_table(slots - 1, BUCKETS, token_reach)
    return table[offset + slots - 1][None, :] == np.arange(BUCKETS)[:, None]


def write_pairs(marks_ref, x_rows, y_rows):
    odd = lax.broadcasted_iota(jnp.int32, (16, 1), 0) >= 8
    one = jnp.ones((16, x_rows.shape[1]), jnp.bfloat16)
    zero = jnp.zeros((16, x_rows.shape[1]), jnp.bfloat16)
    shift = jnp.where(odd, 1.0, 0.0).astype(jnp.bfloat16)
    for at, rows in enumerate((x_rows, y_rows)):
        even = rows - shift
        for b in range(0, BUCKETS, 2):
            begin = (at * BUCKETS + b) * 8
            marks_ref[begin : begin + 16, :] = jnp.where(even == b, one, zero)


def write_marks(marks_ref, x_tile, y_tile, begin=0):
    one = jnp.ones(x_tile.shape, jnp.bfloat16)
    zero = jnp.zeros(x_tile.shape, jnp.bfloat16)
    cols = slice(begin, begin + x_tile.shape[1])
    for b in range(BUCKETS):
        if b == DEAD_BUCKET:
            continue
        marks_ref[b * 16 : b * 16 + 16, cols] = jnp.where(x_tile == b, one, zero)
        marks_ref[512 + b * 16 : 512 + b * 16 + 16, cols] = jnp.where(y_tile == b, one, zero)


def index_kernel(len_ref, box_ref, turned_ref, ix_ref, iy_ref, ix2_ref, iy2_ref):
    place = lax.broadcasted_iota(jnp.int32, ix_ref.shape, 1)
    x_bucket = bucket_index(box_ref[0:1, :] - turned_ref[:, 0:1], coord_top, layout_reach)
    y_bucket = bucket_index(box_ref[1:2, :] - turned_ref[:, 1:2], coord_top, layout_reach)
    x_bucket = jnp.where(place < len_ref[0], x_bucket, DEAD_BUCKET).astype(jnp.float32)
    y_bucket = y_bucket.astype(jnp.float32)
    ix_ref[...] = x_bucket.astype(jnp.bfloat16)
    iy_ref[...] = y_bucket.astype(jnp.bfloat16)
    for twice_ref, value in ((ix2_ref, x_bucket), (iy2_ref, y_bucket)):
        for r in range(0, ix_ref.shape[0], 8):
            part = value[r : r + 8]
            twice_ref[2 * r : 2 * r + 16, :] = jnp.concatenate([part, part]).astype(jnp.bfloat16)


def index_call(length, box):
    slots = box.shape[1]
    tile = pl.BlockSpec((BIAS_TILE, slots), lambda i: (i, 0))
    twice = pl.BlockSpec((2 * BIAS_TILE, slots), lambda i: (i, 0))
    return pl.pallas_call(
        index_kernel,
        grid=(slots // BIAS_TILE,),
        in_specs=[
            pl.BlockSpec(memory_space=pltpu.SMEM),
            pl.BlockSpec((2, slots), lambda i: (0, 0)),
            pl.BlockSpec((BIAS_TILE, 2), lambda i: (i, 0)),
        ],
        out_specs=[tile, tile, twice, twice],
        out_shape=[jax.ShapeDtypeStruct((slots, slots), jnp.bfloat16)] * 2
        + [jax.ShapeDtypeStruct((2 * slots, slots), jnp.bfloat16)] * 2,
        name="index",
        **params_for(1e9, 4e6),
    )(length, box, box.T)


def prepare_kernel(tables_ref, marks_ref, lhs_ref, skew_ref):
    slots = marks_ref.shape[1]
    tables = tables_ref[...]
    rel_row = jnp.dot(
        tables[:, :BUCKETS], marks_ref[...], preferred_element_type=jnp.float32
    )
    for h in range(HEADS):
        wide = jnp.broadcast_to(rel_row[h : h + 1, :], (BIAS_TILE, slots))
        skew = pltpu.roll(wide, 0, 1, stride=1, stride_axis=0)[:, :640]
        skew_ref[h] = skew
    tall, long = HEADS * 8, 2 * BUCKETS * 8
    layout = tables[:, BUCKETS:]
    dead = lax.broadcasted_iota(jnp.int32, layout.shape, 1) == DEAD_BUCKET
    layout = jnp.where(dead, jnp.asarray(masked_score, jnp.bfloat16), layout)
    head_of = lax.broadcasted_iota(jnp.int32, (tall, HEADS), 0) // 8
    pick_head = head_of == lax.broadcasted_iota(jnp.int32, (tall, HEADS), 1)
    bucket_of = lax.broadcasted_iota(jnp.int32, (2 * BUCKETS, long), 1) // 8
    pick_bucket = bucket_of == lax.broadcasted_iota(jnp.int32, (2 * BUCKETS, long), 0)
    by_head = jnp.dot(
        pick_head.astype(jnp.bfloat16), layout, preferred_element_type=jnp.float32
    ).astype(jnp.bfloat16)
    full = jnp.dot(
        by_head, pick_bucket.astype(jnp.bfloat16), preferred_element_type=jnp.float32
    )
    same = (
        lax.broadcasted_iota(jnp.int32, (tall, long), 0) % 8
        == lax.broadcasted_iota(jnp.int32, (tall, long), 1) % 8
    )
    lhs_ref[...] = jnp.where(same, full, 0.0).astype(jnp.bfloat16)


def prepare_call(tables, slots):
    return pl.pallas_call(
        prepare_kernel,
        out_shape=[
            jax.ShapeDtypeStruct((HEADS * 8, 2 * BUCKETS * 8), jnp.bfloat16),
            jax.ShapeDtypeStruct((HEADS, BIAS_TILE, 640), jnp.float32),
        ],
        name="prepare",
        **params_for(1e9, 6e6),
    )(tables, jnp.asarray(rel_marks(slots, 256)).astype(jnp.bfloat16))


def two_at_a_time(ix_ref, iy_ref, first_ref, second_ref, use, joint=1):
    rows, slots = ix_ref.shape
    step = 16 * joint

    def write(ref, r0):
        for at in range(joint):
            here = pl.multiple_of(jnp.minimum(r0 + 16 * at, rows - 16), 16)
            write_marks(ref, ix_ref[pl.ds(here, 16), :], iy_ref[pl.ds(here, 16), :], at * slots)

    write(first_ref, 0)

    def body(t, carry):
        r0 = pl.multiple_of(t * 2 * step, 2 * step)
        write(second_ref, r0 + step)
        use(r0, first_ref)
        write(first_ref, r0 + 2 * step)
        use(pl.multiple_of(r0 + step, step), second_ref)
        return carry

    lax.fori_loop(0, rows // (2 * step), body, 0)


def bias_kernel(first, ix_ref, iy_ref, lhs_ref, skew_ref, *rest):
    bias_ref, first_ref, second_ref = rest[-3:]
    block = pl.program_id(0) + first
    slots = ix_ref.shape[1]
    rows = BIAS_TILE

    def write(ref, r0):
        r0 = pl.multiple_of(jnp.minimum(2 * r0, 2 * rows - 16), 16)
        write_pairs(ref, ix_ref[pl.ds(r0, 16), :], iy_ref[pl.ds(r0, 16), :])

    def use(r0, marks_ref):
        out = jnp.dot(lhs_ref[...], marks_ref[...], preferred_element_type=jnp.float32)
        for c in range(slots // 128):
            shift = pl.multiple_of((jnp.clip(c - block, -2, 2) + 2) * 128, 128)
            cols = slice(c * 128, c * 128 + 128)
            for h in range(HEADS):
                bias_ref[h, pl.ds(r0, 8), cols] = out[
                    h * 8 : h * 8 + 8, cols
                ] + skew_ref[h, pl.ds(r0, 8), pl.ds(shift, 128)]

    write(first_ref, 0)

    def body(t, carry):
        r0 = pl.multiple_of(t * 16, 16)
        write(second_ref, r0 + 8)
        use(r0, first_ref)
        write(first_ref, r0 + 16)
        use(pl.multiple_of(r0 + 8, 8), second_ref)
        return carry

    lax.fori_loop(0, rows // 16, body, 0)


def bias_call(ix, iy, lhs, skew, begin, end, held=None):
    slots = ix.shape[1]
    tile = pl.BlockSpec((2 * BIAS_TILE, slots), lambda i: (i + begin, 0))
    in_specs = [
        tile,
        tile,
        pl.BlockSpec(lhs.shape, lambda i: (0, 0)),
        pl.BlockSpec(skew.shape, lambda i: (0, 0, 0)),
    ]
    args = [ix, iy, lhs, skew]
    aliases = {}
    if held is not None:
        in_specs.append(pl.BlockSpec(memory_space=pl.ANY))
        args.append(held)
        aliases = {4: 0}
    share = (end - begin) * BIAS_TILE / slots
    return pl.pallas_call(
        functools.partial(bias_kernel, begin),
        grid=(end - begin,),
        in_specs=in_specs,
        out_specs=pl.BlockSpec((HEADS, BIAS_TILE, slots), lambda i: (0, i + begin, 0)),
        out_shape=jax.ShapeDtypeStruct((HEADS, slots, slots), jnp.float32),
        scratch_shapes=[pltpu.VMEM((2 * BUCKETS * 8, slots), jnp.bfloat16)] * 2,
        input_output_aliases=aliases,
        name="bias",
        **params_for(34e9 * share, 72e6 * share),
    )(*args)


def own_lanes(h):
    left = lax.broadcasted_iota(jnp.int32, (1, 128), 1) < HEAD_DIM
    return left if h == 0 else jnp.logical_not(left)


def attend_kernel(q_ref, k_ref, v_ref, bias_ref, probs_ref, mixed_ref):
    q, k, v = q_ref[...], k_ref[...], v_ref[...]
    outs = []
    for h in range(2):
        q_own = jnp.where(own_lanes(h), q, jnp.zeros_like(q))
        scores = lax.dot_general(
            q_own, k, (((1,), (1,)), ((), ())), preferred_element_type=jnp.float32
        )
        strips = []
        for r in range(0, q.shape[0], STRIP):
            strip = scores[r : r + STRIP] + bias_ref[h, r : r + STRIP, :]
            top = jnp.max(strip, axis=1, keepdims=True)
            weights = jnp.exp(strip - top)
            total = jnp.sum(weights, axis=1, keepdims=True)
            strips.append((weights * (1.0 / total)).astype(jnp.bfloat16))
        probs = jnp.concatenate(strips, axis=0)
        probs_ref[h] = probs
        outs.append(jnp.dot(probs, v, preferred_element_type=jnp.float32))
    mixed_ref[...] = jnp.where(own_lanes(0), outs[0], outs[1]).astype(jnp.bfloat16)


def attend_call(query, key_rows, value_rows, bias):
    slots, inner = query.shape
    pairs = inner // 128
    tile = min(ROW_TILE, slots)
    rows = pl.BlockSpec((tile, 128), lambda p, i: (i, p))
    square = pl.BlockSpec((2, tile, slots), lambda p, i: (p, i, 0))
    return pl.pallas_call(
        attend_kernel,
        grid=(pairs, slots // tile),
        in_specs=[
            rows,
            pl.BlockSpec((slots, 128), lambda p, i: (0, p)),
            pl.BlockSpec((slots, 128), lambda p, i: (0, p)),
            square,
        ],
        out_specs=[square, rows],
        out_shape=[
            jax.ShapeDtypeStruct((HEADS, slots, slots), jnp.bfloat16),
            jax.ShapeDtypeStruct((slots, inner), jnp.bfloat16),
        ],
        name="attend",
        **params_for(34e9, 100e6),
    )(query, key_rows, value_rows, bias)


def attend_back_kernel(q_ref, k_ref, v_ref, grad_ref, probs_ref, *rest):
    ds_ref, dq_ref, dk_ref, dv_ref, k_sum, v_sum = rest[-6:]
    step = pl.program_id(1)
    q, k, v, grad = q_ref[...], k_ref[...], v_ref[...], grad_ref[...]
    q_turned, grad_turned = q.T, grad.T

    @pl.when(step == 0)
    def _():
        k_sum[...] = jnp.zeros_like(k_sum)
        v_sum[...] = jnp.zeros_like(v_sum)

    outs = []
    for h in range(2):
        grad_own = jnp.where(own_lanes(h), grad, jnp.zeros_like(grad))
        grad_probs = lax.dot_general(
            grad_own, v, (((1,), (1,)), ((), ())), preferred_element_type=jnp.float32
        )
        strips = []
        for r in range(0, q.shape[0], STRIP):
            probs = probs_ref[h, r : r + STRIP, :].astype(jnp.float32)
            terms = probs * grad_probs[r : r + STRIP]
            delta = jnp.sum(terms, axis=1, keepdims=True)
            strips.append((terms - probs * delta).astype(jnp.bfloat16))
        ds = jnp.concatenate(strips, axis=0)
        ds_ref[h] = ds
        outs.append(jnp.dot(ds, k, preferred_element_type=jnp.float32))
        own = slice(h * HEAD_DIM, (h + 1) * HEAD_DIM)
        k_sum[own, :] += jnp.dot(q_turned[own], ds, preferred_element_type=jnp.float32)
        v_sum[own, :] += jnp.dot(
            grad_turned[own], probs_ref[h], preferred_element_type=jnp.float32
        )
    dq_ref[...] = jnp.where(own_lanes(0), outs[0], outs[1]).astype(jnp.bfloat16)

    @pl.when(step == pl.num_programs(1) - 1)
    def _():
        dk_ref[...] = k_sum[...].T.astype(jnp.bfloat16)
        dv_ref[...] = v_sum[...].T.astype(jnp.bfloat16)


def attend_back_call(query, key_rows, value_rows, grad_mixed, probs, begin, end, held=None):
    slots, inner = query.shape
    tile = min(ROW_TILE, slots)
    rows = pl.BlockSpec((tile, 128), lambda p, i: (i, p + begin))
    whole = pl.BlockSpec((slots, 128), lambda p, i: (0, p + begin))
    square = pl.BlockSpec((2, tile, slots), lambda p, i: (p + begin, i, 0))
    args = [query, key_rows, value_rows, grad_mixed, probs]
    in_specs = [rows, whole, whole, rows, square]
    aliases = {}
    if held is not None:
        aliases = {len(args) + at: at for at in range(len(held))}
        in_specs += [pl.BlockSpec(memory_space=pl.ANY)] * len(held)
        args += list(held)
    share = (end - begin) * 128 / inner
    return pl.pallas_call(
        attend_back_kernel,
        grid=(end - begin, slots // tile),
        in_specs=in_specs,
        out_specs=[square, rows, whole, whole],
        out_shape=[jax.ShapeDtypeStruct((HEADS, slots, slots), jnp.bfloat16)]
        + [jax.ShapeDtypeStruct((slots, inner), jnp.bfloat16)] * 3,
        scratch_shapes=[pltpu.VMEM((128, slots), jnp.float32)] * 2,
        input_output_aliases=aliases,
        name="attend_back",
        **params_for(34e9 * share, 72e6 * share),
    )(*args)


def rel_near_marks(slots):
    row = np.arange(BIAS_TILE)[:, None]
    offset = np.arange(640)[None, :] - 256 - row
    bucket = bucket_table(slots - 1, BUCKETS, token_reach)[offset + slots - 1]
    marks = bucket[None, :, :] == np.arange(BUCKETS)[:, None, None]
    marks = marks.reshape(BUCKETS, BIAS_TILE // 16, 16, 640).transpose(1, 0, 2, 3)
    return marks.reshape(BIAS_TILE // 16, BUCKETS * 16, 640)


def table_kernel(
    first, ds_ref, ix_ref, iy_ref, near_ref, out_ref, total, rel_total, first_ref, second_ref
):
    step = pl.program_id(0)
    block = step + first
    slots = ix_ref.shape[1]
    blocks = slots // BIAS_TILE
    heads = ds_ref.shape[0]

    @pl.when(step == 0)
    def _():
        total[...] = jnp.zeros_like(total)
        rel_total[...] = jnp.zeros_like(rel_total)

    begin = jnp.clip(block - 1, 0, blocks - 3)
    lanes = pl.ds(pl.multiple_of(begin * BIAS_TILE, BIAS_TILE), 3 * BIAS_TILE)
    source = pl.ds(
        pl.multiple_of((begin - block + 2) * BIAS_TILE, BIAS_TILE), 3 * BIAS_TILE
    )
    place = lax.broadcasted_iota(jnp.int32, (16, TABLE_JOINT * slots), 1) % slots
    low = (place < begin * BIAS_TILE).astype(jnp.float32).astype(jnp.bfloat16)
    high = (place >= (begin + 3) * BIAS_TILE).astype(jnp.float32).astype(jnp.bfloat16)
    for ref in (first_ref, second_ref):
        ref[DEAD_BUCKET * 16 : DEAD_BUCKET * 16 + 16, :] = low
        ref[(BUCKETS + DEAD_BUCKET) * 16 : (BUCKETS + DEAD_BUCKET) * 16 + 16, :] = high

    def use(r0, marks_ref):
        ds, close, near = [], [], []
        for at in range(TABLE_JOINT):
            here = pl.ds(pl.multiple_of(r0 + 16 * at, 16), 16)
            ds.append(ds_ref[:, here, :].reshape(heads * 16, slots))
            close.append(ds_ref[:, here, lanes].reshape(heads * 16, 3 * BIAS_TILE))
            near.append(near_ref[r0 // 16 + at, :, source])
        total[...] += right_transposed(marks_ref[...], jnp.concatenate(ds, axis=1))
        rel_total[...] += right_transposed(
            jnp.concatenate(near, axis=1), jnp.concatenate(close, axis=1)
        )

    two_at_a_time(ix_ref, iy_ref, first_ref, second_ref, use, TABLE_JOINT)

    @pl.when(step == pl.num_programs(0) - 1)
    def _():
        at = 0
        for ref in (total, rel_total):
            shape = ref.shape
            same = (
                lax.broadcasted_iota(jnp.int32, shape, 0) % 16
                == lax.broadcasted_iota(jnp.int32, shape, 1) % 16
            )
            kept = jnp.where(same, ref[...], 0.0).reshape(shape[0] // 16, 16, shape[1])
            out_ref[at : at + shape[0] // 16, :] = kept.sum(axis=1)
            at += shape[0] // 16


def table_call(ds, ix, iy, begin, end):
    slots = ix.shape[0]
    tile = pl.BlockSpec((BIAS_TILE, slots), lambda i: (i + begin, 0))
    share = (end - begin) * BIAS_TILE / slots
    near = jnp.asarray(rel_near_marks(slots)).astype(jnp.bfloat16)
    marked = 2 * BUCKETS * 16
    return pl.pallas_call(
        functools.partial(table_kernel, begin),
        grid=(end - begin,),
        in_specs=[
            pl.BlockSpec((HEADS, BIAS_TILE, slots), lambda i: (0, i + begin, 0)),
            tile,
            tile,
            pl.BlockSpec(near.shape, lambda i: (0, 0, 0)),
        ],
        out_specs=pl.BlockSpec((3 * BUCKETS, HEADS * 16), lambda i: (0, 0)),
        out_shape=jax.ShapeDtypeStruct((3 * BUCKETS, HEADS * 16), jnp.float32),
        scratch_shapes=[
            pltpu.VMEM((marked, HEADS * 16), jnp.float32),
            pltpu.VMEM((BUCKETS * 16, HEADS * 16), jnp.float32),
            pltpu.VMEM((marked, TABLE_JOINT * slots), jnp.bfloat16),
            pltpu.VMEM((marked, TABLE_JOINT * slots), jnp.bfloat16),
        ],
        name="table_back",
        **params_for(40e9 * share, 40e6 * share),
    )(ds, ix, iy, near)


def table_finish(parts):
    sums = sum(parts).reshape(3, BUCKETS, HEADS, 16).sum(axis=3).transpose(0, 2, 1)
    column = jnp.arange(BUCKETS)[None, :]
    far = sums[:2, :, DEAD_BUCKET : DEAD_BUCKET + 1]
    rel = sums[2] + jnp.where(column == BUCKETS // 2 - 1, far[0], 0.0)
    rel = rel + jnp.where(column == BUCKETS - 1, far[1], 0.0)
    layout = jnp.where(column == DEAD_BUCKET, 0.0, sums[:2])
    return rel, layout[0], layout[1]


def ffn_kernel(
    unit, spots, core_ref, gain_ref, seed_ref, hidden_ref, gate_ref, up_ref, down_ref,
    out_ref, grad_ref, low_ref, dgain_ref, gate_away_ref, gate_stay_ref, up_away_ref,
    up_stay_ref, down_away_ref, down_stay_ref, out_sum, n_ref, turned_ref, ddown_ref,
):
    step = pl.program_id(0)
    slots, width = n_ref.shape
    half = width // 2
    rows = half // len(spots[0])

    def place(refs, spot, value):
        for ref, part in zip(refs, (value[:half], value[half:])):
            for at, to in enumerate(spot):
                ref[to * rows : (to + 1) * rows, :] = part[at * rows : (at + 1) * rows]

    @pl.when(step == 0)
    def _():
        for r in range(0, slots, 64):
            rows_now = hidden_ref[r : r + 64, :]
            out_sum[r : r + 64, :] = rows_now
            n_ref[r : r + 64, :] = norm_apply(rows_now, gain_ref[...]).astype(jnp.bfloat16)
        grad_ref[...] = jnp.zeros_like(grad_ref)
        core = core_ref[0]
        for lanes in range(0, width, 128):
            turned = n_ref[:, lanes : lanes + 128].T
            for part in range(128 // unit):
                group = lanes // unit + part
                first = jnp.where(core == group % 2, half, 0) + group // 2 * unit
                turned_ref[pl.ds(pl.multiple_of(first, 16), unit), :] = turned[
                    part * unit : (part + 1) * unit
                ]

    seed = seed_ref[...]
    w_gate, w_up, w_down = gate_ref[...], up_ref[...], down_ref[...]
    gate = plain_product(n_ref[...], w_gate)
    upper = plain_product(n_ref[...], w_up)
    grad_act = right_transposed(seed, w_down)
    square = gate * gate
    tanh = jnp.tanh(gelu_scale * (gate + 0.044715 * gate * square))
    cdf = 0.5 * (1.0 + tanh)
    gelu = gate * cdf
    slope = cdf + 0.5 * gate * (1.0 - tanh * tanh) * gelu_scale * (1.0 + 3 * 0.044715 * square)
    activated = (gelu * upper).astype(jnp.bfloat16)
    grad_gate = (grad_act * upper * slope).astype(jnp.bfloat16)
    grad_upper = (grad_act * gelu).astype(jnp.bfloat16)
    out_sum[...] += plain_product(activated, w_down)
    grad_ref[...] += right_transposed(
        jnp.concatenate([grad_gate, grad_upper], axis=1), jnp.concatenate([w_gate, w_up], axis=1)
    )
    d_gate = plain_product(turned_ref[...], grad_gate).astype(jnp.bfloat16)
    place((gate_away_ref, gate_stay_ref), spots[0], d_gate)
    d_up = plain_product(turned_ref[...], grad_upper).astype(jnp.bfloat16)
    place((up_away_ref, up_stay_ref), spots[1], d_up)
    tile = w_down.shape[0]
    ddown_ref[pl.ds(pl.multiple_of(step * tile, tile), tile), :] = left_transposed(
        activated, seed
    ).astype(jnp.bfloat16)

    @pl.when(step == pl.num_programs(0) - 1)
    def _():
        gain = gain_ref[...]
        gain_sum = jnp.zeros((1, width), jnp.float32)
        for r in range(0, slots, 64):
            here = slice(r, r + 64)
            out_ref[here, :] = out_sum[here, :].astype(jnp.bfloat16)
            value, grad = hidden_ref[here, :], grad_ref[here, :]
            scale = lax.rsqrt(jnp.mean(value * value, axis=1, keepdims=True) + epsilon)
            turn = value * scale
            gain_sum += jnp.sum(grad * turn, axis=0, keepdims=True)
            grad = grad * gain
            shift = jnp.mean(grad * turn, axis=1, keepdims=True)
            total = seed_ref[here, :].astype(jnp.float32) + scale * (grad - turn * shift)
            grad_ref[here, :] = total
            low_ref[here, :] = total.astype(jnp.bfloat16)
        dgain_ref[...] = gain_sum
        tall = ddown_ref.shape[0] // (2 * len(spots[2]))
        low_bits = unit // rows
        flip = core_ref[0] == 1
        for at, to in enumerate(spots[2]):
            first = (at // low_bits * 2 * low_bits + at % low_bits) * tall
            second = first + low_bits * tall
            zero = ddown_ref[first : first + tall, :]
            one = ddown_ref[second : second + tall, :]
            down_away_ref[to * tall : (to + 1) * tall, :] = jnp.where(flip, zero, one)
            down_stay_ref[to * tall : (to + 1) * tall, :] = jnp.where(flip, one, zero)


def ffn_call(core, unit, spots, gain, seed, hidden, packed, w_down):
    slots, width = hidden.shape
    ff = w_down.shape[0]
    tile = 256
    count = ff // tile
    single = pl.Buffered(1)
    full = pl.BlockSpec((slots, width), lambda f: (0, 0), pipeline_mode=single)
    column = pl.BlockSpec((width // 2, tile), lambda f: (0, f))
    row = pl.BlockSpec((tile, width), lambda f: (f, 0))
    down_half = pl.BlockSpec((ff // 2, width), lambda f: (0, 0), pipeline_mode=single)
    vector = pl.BlockSpec((1, width), lambda f: (0, 0))
    return pl.pallas_call(
        functools.partial(ffn_kernel, unit, spots),
        grid=(count,),
        in_specs=[
            pl.BlockSpec(memory_space=pltpu.SMEM),
            vector,
            full,
            full,
            pl.BlockSpec((width, tile), lambda f: (0, f)),
            pl.BlockSpec((width, tile), lambda f: (0, f + count)),
            row,
        ],
        out_specs=[full, full, full, vector] + [column] * 4 + [down_half] * 2,
        out_shape=[
            jax.ShapeDtypeStruct((slots, width), jnp.bfloat16),
            jax.ShapeDtypeStruct((slots, width), jnp.float32),
            jax.ShapeDtypeStruct((slots, width), jnp.bfloat16),
            jax.ShapeDtypeStruct((1, width), jnp.float32),
        ]
        + [jax.ShapeDtypeStruct((width // 2, ff), jnp.bfloat16)] * 4
        + [jax.ShapeDtypeStruct((ff // 2, width), jnp.bfloat16)] * 2,
        scratch_shapes=[
            pltpu.VMEM((slots, width), jnp.float32),
            pltpu.VMEM((slots, width), jnp.bfloat16),
            pltpu.VMEM((width, slots), jnp.bfloat16),
            pltpu.VMEM((ff, width), jnp.bfloat16),
        ],
        name="ffn",
        **params_for(18 * slots * width * ff, 50e6),
    )(core, gain, seed, hidden, packed, packed, w_down)


class Exchange:
    def __init__(self, mesh):
        self.count = mesh.shape["wide"] * mesh.shape["narrow"]
        self.bits = self.count.bit_length() - 1
        assert self.count == 1 << self.bits
        one, two, three, *tail = [b for b in range(self.bits) if b != CORE_BIT]
        self.orders = (
            [CORE_BIT, one, two] + tail + [three],
            [CORE_BIT, two, three, one] + tail,
            [CORE_BIT, three, one, two] + tail,
        )

    def me(self):
        return lax.axis_index(AXES)

    def mine(self, bit):
        return (self.me() >> bit) & 1

    def swap(self, value, bit):
        pairs = [(d, d ^ (1 << bit)) for d in range(self.count)]
        return lax.ppermute(value, AXES, pairs)

    def spots(self, order):
        held = [b for b in range(self.bits - 1, -1, -1) if b != CORE_BIT]
        steps = self.orders[order][1:]
        last = len(held) - 1
        found = []
        for at in range(1 << len(held)):
            value = {bit: at >> (last - k) & 1 for k, bit in enumerate(held)}
            found.append(sum(value[bit] << (last - k) for k, bit in enumerate(steps)))
        return tuple(found)

    def spread(self, shard):
        copies = jnp.broadcast_to(shard[None], (self.count,) + shard.shape)
        return lax.all_to_all(copies, AXES, 0, 0, tiled=True)

    def sum_small(self, terms):
        return jnp.sum(lax.all_to_all(terms, AXES, 0, 0, tiled=True), axis=0)


class Gather:
    def __init__(self, exchange, shard, order):
        self.exchange = exchange
        self.value = shard[None]
        self.steps = list(reversed(exchange.orders[order]))
        self.offsets = [0]
        self.flight = None

    def done(self):
        return not self.steps

    def go(self):
        self.flight = self.exchange.swap(self.value, self.steps[0])

    def land(self):
        bit = self.steps.pop(0)
        other, self.flight = self.flight, None
        self.offsets += [offset | 1 << bit for offset in self.offsets]
        if self.steps:
            self.value = jnp.concatenate([self.value, other], axis=0)
        else:
            self.other = other


def project_kernel(offsets, me_ref, x_ref, *refs):
    count = len(offsets)
    halves, outs, scratch = refs[: 2 * count], refs[2 * count : 4 * count], refs[4 * count]
    me = me_ref[0]
    for at in range(count):
        value_ref, other_ref = halves[2 * at : 2 * at + 2]
        out_ref, full_ref = outs[2 * at : 2 * at + 2]
        places, rows, _ = value_ref.shape
        for place, offset in enumerate(offsets[at]):
            part = value_ref[place] if place < places else other_ref[place - places]
            begin = pl.multiple_of((me ^ offset) * rows, rows)
            scratch[at, pl.ds(begin, rows), :] = part
        full_ref[...] = scratch[at]
        out_ref[...] = plain_product(x_ref[...], scratch[at]).astype(jnp.bfloat16)


def project_call(exchange, normed, tasks):
    places, rows, inner = tasks[0].value.shape
    slots, width = normed.shape
    if rows % 16:
        fulls, outs = [], []
        for task in tasks:
            held = jnp.concatenate([task.value, task.other], axis=0)
            place_of = np.argsort(np.asarray(task.offsets))
            spots = jnp.asarray(place_of)[exchange.me() ^ jnp.arange(exchange.count)]
            fulls.append(jnp.take(held, spots, axis=0).reshape(width, inner))
            outs.append(plain_product(normed, fulls[-1]).astype(jnp.bfloat16))
        return outs, fulls
    tile = 256
    part = pl.BlockSpec((places, rows, tile), lambda n: (0, 0, n))
    column = pl.BlockSpec((slots, tile), lambda n: (0, n))
    full = pl.BlockSpec((width, tile), lambda n: (0, n))
    results = pl.pallas_call(
        functools.partial(project_kernel, tuple(tuple(task.offsets) for task in tasks)),
        grid=(inner // tile,),
        in_specs=[
            pl.BlockSpec(memory_space=pltpu.SMEM),
            pl.BlockSpec((slots, width), lambda n: (0, 0)),
        ]
        + [part] * (2 * len(tasks)),
        out_specs=[column, full] * len(tasks),
        out_shape=[
            jax.ShapeDtypeStruct((slots, inner), jnp.bfloat16),
            jax.ShapeDtypeStruct((width, inner), jnp.bfloat16),
        ]
        * len(tasks),
        scratch_shapes=[pltpu.VMEM((len(tasks), width, tile), jnp.bfloat16)],
        name="project",
        **params_for(2 * len(tasks) * slots * width * inner, 20e6),
    )(
        exchange.me().astype(jnp.int32).reshape(1),
        normed,
        *[half for task in tasks for half in (task.value, task.other)],
    )
    return results[0::2], results[1::2]


class Scatter:
    def __init__(self, exchange, terms, order, away=None):
        self.exchange = exchange
        self.held = list(range(exchange.bits - 1, -1, -1))
        if away is not None:
            self.held = exchange.orders[order][1:]
        dims = (2,) * len(self.held)
        rows = terms.shape[0] >> len(self.held)
        self.value = terms.reshape(dims + (rows,) + terms.shape[1:])
        self.away = None if away is None else away.reshape(self.value.shape)
        self.steps = list(exchange.orders[order])
        self.flight = None

    def done(self):
        return not self.steps

    def go(self):
        bit = self.steps[0]
        if self.away is not None:
            self.flight = self.exchange.swap(self.away, bit)
            return
        self.spot = self.held.index(bit)
        away = lax.dynamic_index_in_dim(
            self.value, 1 - self.exchange.mine(bit), self.spot, keepdims=False
        )
        self.flight = self.exchange.swap(away, bit)

    def land(self):
        bit = self.steps.pop(0)
        other, self.flight = self.flight, None
        stay = self.value
        if self.away is None:
            stay = lax.dynamic_index_in_dim(
                self.value, self.exchange.mine(bit), self.spot, keepdims=False
            )
            self.held.pop(self.spot)
        self.away = None
        value = stay.astype(jnp.float32) + other.astype(jnp.float32)
        if self.steps:
            value = value.astype(jnp.bfloat16)
        self.value = value


class Traffic:
    limit = 5

    def __init__(self):
        self.tasks = []

    def add(self, *tasks):
        self.tasks += tasks
        self.send()

    def send(self):
        busy = sum(task.flight is not None for task in self.tasks)
        for task in self.tasks:
            if task.flight is None and busy < self.limit:
                task.go()
                busy += 1

    def step(self, *work):
        flying = [task for task in self.tasks if task.flight is not None]
        work, flights = lax.optimization_barrier((work, [task.flight for task in flying]))
        for task, flight in zip(flying, flights):
            task.flight = flight
            task.land()
        self.tasks = [task for task in self.tasks if not task.done()]
        self.send()
        return work[0] if len(work) == 1 else work


def norm_apply(values, gain):
    return values * lax.rsqrt(jnp.mean(values * values, axis=-1, keepdims=True) + epsilon) * gain


def layer(
    exchange, inputs, norm_first, w_query, w_key, w_value, w_out, rel_table, x_table, y_table,
    norm_second, w_gate, w_up, w_down, lengths, boxes, cotangent,
):
    seq_count, slots, width = inputs.shape
    inner = w_query.shape[1]
    count = exchange.count
    entries = rel_table.shape[0]
    span = norm_first.shape[0]

    rows = inputs.reshape(slots, width).astype(jnp.float32)
    seed = cotangent.reshape(slots, width)
    traffic = Traffic()
    qkv_tasks = [
        Gather(exchange, shard, order) for order, shard in enumerate((w_query, w_key, w_value))
    ]
    traffic.add(*qkv_tasks)
    longest = max(span, entries)
    small = exchange.spread(
        jnp.stack(
            [
                jnp.pad(part, (0, longest - part.shape[0]))
                for part in (norm_first, norm_second, rel_table, x_table, y_table)
            ]
        )
    ).reshape(count, 5, longest)
    packed = lax.all_gather(
        jnp.concatenate([w_gate, w_up, w_out], axis=1), AXES, axis=0, tiled=True
    )
    down_full = lax.all_gather(w_down, AXES, axis=0, tiled=True)
    ix, iy, ix_twice, iy_twice = index_call(lengths, traffic.step(boxes)[0])
    gain_one = small[:, 0, :span].reshape(-1).astype(jnp.float32)
    gain_two = small[:, 1, :span].reshape(-1).astype(jnp.float32)
    tables = jnp.concatenate(
        [small[:, 2 + at, :entries].reshape(HEADS, BUCKETS) for at in range(3)], axis=1
    )
    lhs, skew = prepare_call(tables, slots)
    blocks = slots // BIAS_TILE
    bias = None
    cuts = [0, blocks // 4, blocks // 4 * 3, blocks] + [blocks] * (exchange.bits - 5)
    for begin, end in zip(cuts[:-1], cuts[1:]):
        if bias is None:
            lhs = traffic.step(lhs)
        else:
            lhs, bias = traffic.step(lhs, bias)
        if end > begin:
            bias = bias_call(ix_twice, iy_twice, lhs, skew, begin, end, bias)
    normed_one = norm_apply(rows, gain_one).astype(jnp.bfloat16)
    normed_one, bias = traffic.step(normed_one, bias)
    projected, fulls = project_call(exchange, normed_one, qkv_tasks)
    query, key_rows, value_rows = projected
    query_full, key_full, value_full = fulls
    probs, mixed = attend_call(query, key_rows, value_rows, bias)
    out_full = packed[:, 2 * w_gate.shape[1] :]
    hidden = rows + plain_product(mixed, out_full)
    core = exchange.mine(CORE_BIT).astype(jnp.int32).reshape(1)
    unit = width // count << CORE_BIT
    spots = tuple(exchange.spots(order) for order in range(3))
    output, grad_hidden, branch_low, grad_gain_two, *halves = ffn_call(
        core, unit, spots, gain_two.reshape(1, -1), seed, hidden, packed, down_full
    )
    ffn_tasks = [
        Scatter(exchange, halves[2 * at + 1], at, halves[2 * at]) for at in range(3)
    ]
    traffic.add(*ffn_tasks)
    d_out = left_transposed(mixed, branch_low).astype(jnp.bfloat16)
    grad_mixed = right_transposed(branch_low, out_full).astype(jnp.bfloat16)
    grad_mixed, d_out = traffic.step(grad_mixed, d_out)
    pairs = inner // 128
    cuts = (0, pairs)
    back = None
    for begin, end in zip(cuts[:-1], cuts[1:]):
        back = attend_back_call(
            query, key_rows, value_rows, grad_mixed, probs, begin, end, back
        )
        back = traffic.step(back)
    ds, dq, dk, dv = back
    d_weights = [left_transposed(normed_one, part).astype(jnp.bfloat16) for part in (dq, dk, dv)]
    grad_normed_one = (
        right_transposed(dq, query_full)
        + right_transposed(dk, key_full)
        + right_transposed(dv, value_full)
    )
    grad_normed_one, d_weights = traffic.step(grad_normed_one, d_weights)
    half = width // 2
    d_weights[0] = jnp.concatenate([d_weights[0], d_out[:, :half]], axis=1)
    d_weights[1] = jnp.concatenate([d_weights[1], d_out[:, half:]], axis=1)
    w_tasks = [Scatter(exchange, part, at) for at, part in enumerate(d_weights)]
    traffic.add(*w_tasks)
    unused_one, norm_one_pull = jax.vjp(norm_apply, rows, gain_one)
    rows_part, grad_gain_one = norm_one_pull(grad_normed_one)
    grad_inputs = (grad_hidden + rows_part).reshape(inputs.shape)
    grad_gain_one, ix = traffic.step(grad_gain_one, ix)
    parts = []
    pieces = 3
    for piece in range(pieces):
        begin, end = piece * blocks // pieces, (piece + 1) * blocks // pieces
        parts.append(table_call(ds, ix, iy, begin, end))
        ix, parts = traffic.step(ix, parts)
    grad_rel, grad_x, grad_y = table_finish(parts)
    g_small = exchange.sum_small(
        jnp.concatenate(
            [
                part.reshape(count, -1)
                for part in (grad_gain_one, grad_gain_two, grad_rel, grad_x, grad_y)
            ],
            axis=1,
        )
    )
    while traffic.tasks:
        g_small = traffic.step(g_small)
    g_gate, g_up, g_down = (task.value for task in ffn_tasks)
    edges = [0, span, 2 * span, 2 * span + entries, 2 * span + 2 * entries, g_small.shape[0]]
    g_small = [g_small[a:b] for a, b in zip(edges[:-1], edges[1:])]
    return (
        output.reshape(inputs.shape),
        grad_inputs,
        g_small[0],
        w_tasks[0].value[:, :inner],
        w_tasks[1].value[:, :inner],
        w_tasks[2].value,
        jnp.concatenate([task.value[:, inner:] for task in w_tasks[:2]], axis=1),
        g_small[2],
        g_small[3],
        g_small[4],
        g_small[1],
        g_gate,
        g_up,
        g_down,
    )


def solution(mesh):
    exchange = Exchange(mesh)
    vector, matrix, cube = P(AXES), P(AXES, None), P(AXES, None, None)
    in_specs = (
        (cube, vector)
        + (matrix,) * 4
        + (vector,) * 4
        + (matrix,) * 3
        + (vector, cube, cube)
    )
    out_specs = (cube, cube, vector) + (matrix,) * 4 + (vector,) * 4 + (matrix,) * 3

    def local(*args):
        return layer(exchange, *args)

    return jax.shard_map(local, mesh=mesh, in_specs=in_specs, out_specs=out_specs, check_vma=False)
```

```python
import functools

import jax
import jax.numpy as jnp
import numpy as np
from jax import lax
from jax.experimental import pallas as pl
from jax.experimental.pallas import tpu as pltpu
from jax.sharding import PartitionSpec as P

HEADS = 16
HEAD_DIM = 64
BUCKETS = 32
AXES = ("wide", "narrow")

epsilon = 1e-06
coord_top = 1000
token_reach = 128
layout_reach = 256
masked_score = -1e30
gelu_scale = 0.7978845608028654

VMEM_LIMIT = 60 * 2**20
ROW_TILE = 1024
STRIP = 16
BIAS_TILE = 128
DEAD_BUCKET = 16
CORE_BIT = 1
TABLE_JOINT = 4


def params_for(flops, moved):
    return dict(
        compiler_params=pltpu.CompilerParams(vmem_limit_bytes=VMEM_LIMIT),
        cost_estimate=pl.CostEstimate(
            flops=int(flops), bytes_accessed=int(moved), transcendentals=0
        ),
    )


def plain_product(left, right):
    return jnp.dot(left, right, preferred_element_type=jnp.float32)


def left_transposed(left, right):
    return lax.dot_general(
        left, right, (((0,), (0,)), ((), ())), preferred_element_type=jnp.float32
    )


def right_transposed(left, right):
    return lax.dot_general(
        left, right, (((1,), (1,)), ((), ())), preferred_element_type=jnp.float32
    )


def bucket_table(span, buckets, reach):
    offsets = np.arange(-span, span + 1)
    half = buckets // 2
    exact = half // 2
    side = np.where(offsets > 0, half, 0)
    distance = np.abs(offsets)
    safe = np.maximum(distance, 1)
    large = exact + (np.log(safe / exact) / np.log(reach / exact) * (half - exact)).astype(np.int64)
    large = np.minimum(large, half - 1)
    return side + np.where(distance < exact, distance, large)


def magnitude_steps(span, reach):
    half = BUCKETS // 2
    exact = half // 2
    offsets = np.arange(span + 1)
    table = bucket_table(span, BUCKETS, reach)[span:]
    magnitude = table - np.where(offsets > 0, half, 0)
    steps = []
    for level in range(exact + 1, half):
        if (magnitude >= level).any():
            steps.append(int(np.argmax(magnitude >= level)))
    return steps


def bucket_index(offset, span, reach):
    half = BUCKETS // 2
    exact = half // 2
    distance = jnp.abs(offset)
    edges = magnitude_steps(span, reach)
    edges = [exact] + edges + [2 * span] * (exact - 1 - len(edges))

    def search(low, high):
        if high - low == 1:
            return low
        middle = (low + high) // 2
        return jnp.where(distance >= edges[middle], search(middle, high), search(low, middle))

    magnitude = jnp.where(distance < exact, distance, exact + search(0, len(edges)))
    return magnitude + jnp.where(offset > 0, half, 0)


def rel_marks(slots, zero):
    places = np.arange(slots)
    offset = np.where(places < 768, places - zero, -300)
    table = bucket_table(slots - 1, BUCKETS, token_reach)
    return table[offset + slots - 1][None, :] == np.arange(BUCKETS)[:, None]


def write_pairs(marks_ref, x_rows, y_rows):
    odd = lax.broadcasted_iota(jnp.int32, (16, 1), 0) >= 8
    one = jnp.ones((16, x_rows.shape[1]), jnp.bfloat16)
    zero = jnp.zeros((16, x_rows.shape[1]), jnp.bfloat16)
    shift = jnp.where(odd, 1.0, 0.0).astype(jnp.bfloat16)
    for at, rows in enumerate((x_rows, y_rows)):
        even = rows - shift
        for b in range(0, BUCKETS, 2):
            begin = (at * BUCKETS + b) * 8
            marks_ref[begin : begin + 16, :] = jnp.where(even == b, one, zero)


def write_marks(marks_ref, x_tile, y_tile, begin=0):
    one = jnp.ones(x_tile.shape, jnp.bfloat16)
    zero = jnp.zeros(x_tile.shape, jnp.bfloat16)
    cols = slice(begin, begin + x_tile.shape[1])
    for b in range(BUCKETS):
        if b == DEAD_BUCKET:
            continue
        marks_ref[b * 16 : b * 16 + 16, cols] = jnp.where(x_tile == b, one, zero)
        marks_ref[512 + b * 16 : 512 + b * 16 + 16, cols] = jnp.where(y_tile == b, one, zero)


def index_kernel(len_ref, box_ref, turned_ref, ix_ref, iy_ref, ix2_ref, iy2_ref):
    place = lax.broadcasted_iota(jnp.int32, ix_ref.shape, 1)
    x_bucket = bucket_index(box_ref[0:1, :] - turned_ref[:, 0:1], coord_top, layout_reach)
    y_bucket = bucket_index(box_ref[1:2, :] - turned_ref[:, 1:2], coord_top, layout_reach)
    x_bucket = jnp.where(place < len_ref[0], x_bucket, DEAD_BUCKET).astype(jnp.float32)
    y_bucket = y_bucket.astype(jnp.float32)
    ix_ref[...] = x_bucket.astype(jnp.bfloat16)
    iy_ref[...] = y_bucket.astype(jnp.bfloat16)
    for twice_ref, value in ((ix2_ref, x_bucket), (iy2_ref, y_bucket)):
        for r in range(0, ix_ref.shape[0], 8):
            part = value[r : r + 8]
            twice_ref[2 * r : 2 * r + 16, :] = jnp.concatenate([part, part]).astype(jnp.bfloat16)


def index_call(length, box):
    slots = box.shape[1]
    tile = pl.BlockSpec((BIAS_TILE, slots), lambda i: (i, 0))
    twice = pl.BlockSpec((2 * BIAS_TILE, slots), lambda i: (i, 0))
    return pl.pallas_call(
        index_kernel,
        grid=(slots // BIAS_TILE,),
        in_specs=[
            pl.BlockSpec(memory_space=pltpu.SMEM),
            pl.BlockSpec((2, slots), lambda i: (0, 0)),
            pl.BlockSpec((BIAS_TILE, 2), lambda i: (i, 0)),
        ],
        out_specs=[tile, tile, twice, twice],
        out_shape=[jax.ShapeDtypeStruct((slots, slots), jnp.bfloat16)] * 2
        + [jax.ShapeDtypeStruct((2 * slots, slots), jnp.bfloat16)] * 2,
        name="index",
        **params_for(1e9, 4e6),
    )(length, box, box.T)


def prepare_kernel(tables_ref, marks_ref, lhs_ref, skew_ref):
    slots = marks_ref.shape[1]
    tables = tables_ref[...]
    rel_row = jnp.dot(
        tables[:, :BUCKETS], marks_ref[...], preferred_element_type=jnp.float32
    )
    for h in range(HEADS):
        wide = jnp.broadcast_to(rel_row[h : h + 1, :], (BIAS_TILE, slots))
        skew = pltpu.roll(wide, 0, 1, stride=1, stride_axis=0)[:, :640]
        skew_ref[h] = skew
    tall, long = HEADS * 8, 2 * BUCKETS * 8
    layout = tables[:, BUCKETS:]
    dead = lax.broadcasted_iota(jnp.int32, layout.shape, 1) == DEAD_BUCKET
    layout = jnp.where(dead, jnp.asarray(masked_score, jnp.bfloat16), layout)
    head_of = lax.broadcasted_iota(jnp.int32, (tall, HEADS), 0) // 8
    pick_head = head_of == lax.broadcasted_iota(jnp.int32, (tall, HEADS), 1)
    bucket_of = lax.broadcasted_iota(jnp.int32, (2 * BUCKETS, long), 1) // 8
    pick_bucket = bucket_of == lax.broadcasted_iota(jnp.int32, (2 * BUCKETS, long), 0)
    by_head = jnp.dot(
        pick_head.astype(jnp.bfloat16), layout, preferred_element_type=jnp.float32
    ).astype(jnp.bfloat16)
    full = jnp.dot(
        by_head, pick_bucket.astype(jnp.bfloat16), preferred_element_type=jnp.float32
    )
    same = (
        lax.broadcasted_iota(jnp.int32, (tall, long), 0) % 8
        == lax.broadcasted_iota(jnp.int32, (tall, long), 1) % 8
    )
    lhs_ref[...] = jnp.where(same, full, 0.0).astype(jnp.bfloat16)


def prepare_call(tables, slots):
    return pl.pallas_call(
        prepare_kernel,
        out_shape=[
            jax.ShapeDtypeStruct((HEADS * 8, 2 * BUCKETS * 8), jnp.bfloat16),
            jax.ShapeDtypeStruct((HEADS, BIAS_TILE, 640), jnp.float32),
        ],
        name="prepare",
        **params_for(1e9, 6e6),
    )(tables, jnp.asarray(rel_marks(slots, 256)).astype(jnp.bfloat16))


def two_at_a_time(ix_ref, iy_ref, first_ref, second_ref, use, joint=1):
    rows, slots = ix_ref.shape
    step = 16 * joint

    def write(ref, r0):
        for at in range(joint):
            here = pl.multiple_of(jnp.minimum(r0 + 16 * at, rows - 16), 16)
            write_marks(ref, ix_ref[pl.ds(here, 16), :], iy_ref[pl.ds(here, 16), :], at * slots)

    write(first_ref, 0)

    def body(t, carry):
        r0 = pl.multiple_of(t * 2 * step, 2 * step)
        write(second_ref, r0 + step)
        use(r0, first_ref)
        write(first_ref, r0 + 2 * step)
        use(pl.multiple_of(r0 + step, step), second_ref)
        return carry

    lax.fori_loop(0, rows // (2 * step), body, 0)


def bias_kernel(first, ix_ref, iy_ref, lhs_ref, skew_ref, *rest):
    bias_ref, first_ref, second_ref = rest[-3:]
    block = pl.program_id(0) + first
    slots = ix_ref.shape[1]
    rows = BIAS_TILE

    def write(ref, r0):
        r0 = pl.multiple_of(jnp.minimum(2 * r0, 2 * rows - 16), 16)
        write_pairs(ref, ix_ref[pl.ds(r0, 16), :], iy_ref[pl.ds(r0, 16), :])

    def use(r0, marks_ref):
        out = jnp.dot(lhs_ref[...], marks_ref[...], preferred_element_type=jnp.float32)
        for c in range(slots // 128):
            shift = pl.multiple_of((jnp.clip(c - block, -2, 2) + 2) * 128, 128)
            cols = slice(c * 128, c * 128 + 128)
            for h in range(HEADS):
                bias_ref[h, pl.ds(r0, 8), cols] = out[
                    h * 8 : h * 8 + 8, cols
                ] + skew_ref[h, pl.ds(r0, 8), pl.ds(shift, 128)]

    write(first_ref, 0)

    def body(t, carry):
        r0 = pl.multiple_of(t * 16, 16)
        write(second_ref, r0 + 8)
        use(r0, first_ref)
        write(first_ref, r0 + 16)
        use(pl.multiple_of(r0 + 8, 8), second_ref)
        return carry

    lax.fori_loop(0, rows // 16, body, 0)


def bias_call(ix, iy, lhs, skew, begin, end, held=None):
    slots = ix.shape[1]
    tile = pl.BlockSpec((2 * BIAS_TILE, slots), lambda i: (i + begin, 0))
    in_specs = [
        tile,
        tile,
        pl.BlockSpec(lhs.shape, lambda i: (0, 0)),
        pl.BlockSpec(skew.shape, lambda i: (0, 0, 0)),
    ]
    args = [ix, iy, lhs, skew]
    aliases = {}
    if held is not None:
        in_specs.append(pl.BlockSpec(memory_space=pl.ANY))
        args.append(held)
        aliases = {4: 0}
    share = (end - begin) * BIAS_TILE / slots
    return pl.pallas_call(
        functools.partial(bias_kernel, begin),
        grid=(end - begin,),
        in_specs=in_specs,
        out_specs=pl.BlockSpec((HEADS, BIAS_TILE, slots), lambda i: (0, i + begin, 0)),
        out_shape=jax.ShapeDtypeStruct((HEADS, slots, slots), jnp.float32),
        scratch_shapes=[pltpu.VMEM((2 * BUCKETS * 8, slots), jnp.bfloat16)] * 2,
        input_output_aliases=aliases,
        name="bias",
        **params_for(34e9 * share, 72e6 * share),
    )(*args)


def own_lanes(h):
    left = lax.broadcasted_iota(jnp.int32, (1, 128), 1) < HEAD_DIM
    return left if h == 0 else jnp.logical_not(left)


def attend_kernel(q_ref, k_ref, v_ref, bias_ref, probs_ref, mixed_ref):
    q, k, v = q_ref[...], k_ref[...], v_ref[...]
    outs = []
    for h in range(2):
        q_own = jnp.where(own_lanes(h), q, jnp.zeros_like(q))
        scores = lax.dot_general(
            q_own, k, (((1,), (1,)), ((), ())), preferred_element_type=jnp.float32
        )
        strips = []
        for r in range(0, q.shape[0], STRIP):
            strip = scores[r : r + STRIP] + bias_ref[h, r : r + STRIP, :]
            top = jnp.max(strip, axis=1, keepdims=True)
            weights = jnp.exp(strip - top)
            total = jnp.sum(weights, axis=1, keepdims=True)
            strips.append((weights * (1.0 / total)).astype(jnp.bfloat16))
        probs = jnp.concatenate(strips, axis=0)
        probs_ref[h] = probs
        outs.append(jnp.dot(probs, v, preferred_element_type=jnp.float32))
    mixed_ref[...] = jnp.where(own_lanes(0), outs[0], outs[1]).astype(jnp.bfloat16)


def attend_call(query, key_rows, value_rows, bias):
    slots, inner = query.shape
    pairs = inner // 128
    tile = min(ROW_TILE, slots)
    rows = pl.BlockSpec((tile, 128), lambda p, i: (i, p))
    square = pl.BlockSpec((2, tile, slots), lambda p, i: (p, i, 0))
    return pl.pallas_call(
        attend_kernel,
        grid=(pairs, slots // tile),
        in_specs=[
            rows,
            pl.BlockSpec((slots, 128), lambda p, i: (0, p)),
            pl.BlockSpec((slots, 128), lambda p, i: (0, p)),
            square,
        ],
        out_specs=[square, rows],
        out_shape=[
            jax.ShapeDtypeStruct((HEADS, slots, slots), jnp.bfloat16),
            jax.ShapeDtypeStruct((slots, inner), jnp.bfloat16),
        ],
        name="attend",
        **params_for(34e9, 100e6),
    )(query, key_rows, value_rows, bias)


def attend_back_kernel(q_ref, k_ref, v_ref, grad_ref, probs_ref, *rest):
    ds_ref, dq_ref, dk_ref, dv_ref, k_sum, v_sum = rest[-6:]
    step = pl.program_id(1)
    q, k, v, grad = q_ref[...], k_ref[...], v_ref[...], grad_ref[...]
    q_turned, grad_turned = q.T, grad.T

    @pl.when(step == 0)
    def _():
        k_sum[...] = jnp.zeros_like(k_sum)
        v_sum[...] = jnp.zeros_like(v_sum)

    outs = []
    for h in range(2):
        grad_own = jnp.where(own_lanes(h), grad, jnp.zeros_like(grad))
        grad_probs = lax.dot_general(
            grad_own, v, (((1,), (1,)), ((), ())), preferred_element_type=jnp.float32
        )
        strips = []
        for r in range(0, q.shape[0], STRIP):
            probs = probs_ref[h, r : r + STRIP, :].astype(jnp.float32)
            terms = probs * grad_probs[r : r + STRIP]
            delta = jnp.sum(terms, axis=1, keepdims=True)
            strips.append((terms - probs * delta).astype(jnp.bfloat16))
        ds = jnp.concatenate(strips, axis=0)
        ds_ref[h] = ds
        outs.append(jnp.dot(ds, k, preferred_element_type=jnp.float32))
        own = slice(h * HEAD_DIM, (h + 1) * HEAD_DIM)
        k_sum[own, :] += jnp.dot(q_turned[own], ds, preferred_element_type=jnp.float32)
        v_sum[own, :] += jnp.dot(
            grad_turned[own], probs_ref[h], preferred_element_type=jnp.float32
        )
    dq_ref[...] = jnp.where(own_lanes(0), outs[0], outs[1]).astype(jnp.bfloat16)

    @pl.when(step == pl.num_programs(1) - 1)
    def _():
        dk_ref[...] = k_sum[...].T.astype(jnp.bfloat16)
        dv_ref[...] = v_sum[...].T.astype(jnp.bfloat16)


def attend_back_call(query, key_rows, value_rows, grad_mixed, probs, begin, end, held=None):
    slots, inner = query.shape
    tile = min(ROW_TILE, slots)
    rows = pl.BlockSpec((tile, 128), lambda p, i: (i, p + begin))
    whole = pl.BlockSpec((slots, 128), lambda p, i: (0, p + begin))
    square = pl.BlockSpec((2, tile, slots), lambda p, i: (p + begin, i, 0))
    args = [query, key_rows, value_rows, grad_mixed, probs]
    in_specs = [rows, whole, whole, rows, square]
    aliases = {}
    if held is not None:
        aliases = {len(args) + at: at for at in range(len(held))}
        in_specs += [pl.BlockSpec(memory_space=pl.ANY)] * len(held)
        args += list(held)
    share = (end - begin) * 128 / inner
    return pl.pallas_call(
        attend_back_kernel,
        grid=(end - begin, slots // tile),
        in_specs=in_specs,
        out_specs=[square, rows, whole, whole],
        out_shape=[jax.ShapeDtypeStruct((HEADS, slots, slots), jnp.bfloat16)]
        + [jax.ShapeDtypeStruct((slots, inner), jnp.bfloat16)] * 3,
        scratch_shapes=[pltpu.VMEM((128, slots), jnp.float32)] * 2,
        input_output_aliases=aliases,
        name="attend_back",
        **params_for(34e9 * share, 72e6 * share),
    )(*args)


def rel_near_marks(slots):
    row = np.arange(BIAS_TILE)[:, None]
    offset = np.arange(640)[None, :] - 256 - row
    bucket = bucket_table(slots - 1, BUCKETS, token_reach)[offset + slots - 1]
    marks = bucket[None, :, :] == np.arange(BUCKETS)[:, None, None]
    marks = marks.reshape(BUCKETS, BIAS_TILE // 16, 16, 640).transpose(1, 0, 2, 3)
    return marks.reshape(BIAS_TILE // 16, BUCKETS * 16, 640)


def table_kernel(
    first, ds_ref, ix_ref, iy_ref, near_ref, out_ref, total, rel_total, first_ref, second_ref
):
    step = pl.program_id(0)
    block = step + first
    slots = ix_ref.shape[1]
    blocks = slots // BIAS_TILE
    heads = ds_ref.shape[0]

    @pl.when(step == 0)
    def _():
        total[...] = jnp.zeros_like(total)
        rel_total[...] = jnp.zeros_like(rel_total)

    begin = jnp.clip(block - 1, 0, blocks - 3)
    lanes = pl.ds(pl.multiple_of(begin * BIAS_TILE, BIAS_TILE), 3 * BIAS_TILE)
    source = pl.ds(
        pl.multiple_of((begin - block + 2) * BIAS_TILE, BIAS_TILE), 3 * BIAS_TILE
    )
    place = lax.broadcasted_iota(jnp.int32, (16, TABLE_JOINT * slots), 1) % slots
    low = (place < begin * BIAS_TILE).astype(jnp.float32).astype(jnp.bfloat16)
    high = (place >= (begin + 3) * BIAS_TILE).astype(jnp.float32).astype(jnp.bfloat16)
    for ref in (first_ref, second_ref):
        ref[DEAD_BUCKET * 16 : DEAD_BUCKET * 16 + 16, :] = low
        ref[(BUCKETS + DEAD_BUCKET) * 16 : (BUCKETS + DEAD_BUCKET) * 16 + 16, :] = high

    def use(r0, marks_ref):
        ds, close, near = [], [], []
        for at in range(TABLE_JOINT):
            here = pl.ds(pl.multiple_of(r0 + 16 * at, 16), 16)
            ds.append(ds_ref[:, here, :].reshape(heads * 16, slots))
            close.append(ds_ref[:, here, lanes].reshape(heads * 16, 3 * BIAS_TILE))
            near.append(near_ref[r0 // 16 + at, :, source])
        total[...] += right_transposed(marks_ref[...], jnp.concatenate(ds, axis=1))
        rel_total[...] += right_transposed(
            jnp.concatenate(near, axis=1), jnp.concatenate(close, axis=1)
        )

    two_at_a_time(ix_ref, iy_ref, first_ref, second_ref, use, TABLE_JOINT)

    @pl.when(step == pl.num_programs(0) - 1)
    def _():
        at = 0
        for ref in (total, rel_total):
            shape = ref.shape
            same = (
                lax.broadcasted_iota(jnp.int32, shape, 0) % 16
                == lax.broadcasted_iota(jnp.int32, shape, 1) % 16
            )
            kept = jnp.where(same, ref[...], 0.0).reshape(shape[0] // 16, 16, shape[1])
            out_ref[at : at + shape[0] // 16, :] = kept.sum(axis=1)
            at += shape[0] // 16


def table_call(ds, ix, iy, begin, end):
    slots = ix.shape[0]
    tile = pl.BlockSpec((BIAS_TILE, slots), lambda i: (i + begin, 0))
    share = (end - begin) * BIAS_TILE / slots
    near = jnp.asarray(rel_near_marks(slots)).astype(jnp.bfloat16)
    marked = 2 * BUCKETS * 16
    return pl.pallas_call(
        functools.partial(table_kernel, begin),
        grid=(end - begin,),
        in_specs=[
            pl.BlockSpec((HEADS, BIAS_TILE, slots), lambda i: (0, i + begin, 0)),
            tile,
            tile,
            pl.BlockSpec(near.shape, lambda i: (0, 0, 0)),
        ],
        out_specs=pl.BlockSpec((3 * BUCKETS, HEADS * 16), lambda i: (0, 0)),
        out_shape=jax.ShapeDtypeStruct((3 * BUCKETS, HEADS * 16), jnp.float32),
        scratch_shapes=[
            pltpu.VMEM((marked, HEADS * 16), jnp.float32),
            pltpu.VMEM((BUCKETS * 16, HEADS * 16), jnp.float32),
            pltpu.VMEM((marked, TABLE_JOINT * slots), jnp.bfloat16),
            pltpu.VMEM((marked, TABLE_JOINT * slots), jnp.bfloat16),
        ],
        name="table_back",
        **params_for(40e9 * share, 40e6 * share),
    )(ds, ix, iy, near)


def table_finish(parts):
    sums = sum(parts).reshape(3, BUCKETS, HEADS, 16).sum(axis=3).transpose(0, 2, 1)
    column = jnp.arange(BUCKETS)[None, :]
    far = sums[:2, :, DEAD_BUCKET : DEAD_BUCKET + 1]
    rel = sums[2] + jnp.where(column == BUCKETS // 2 - 1, far[0], 0.0)
    rel = rel + jnp.where(column == BUCKETS - 1, far[1], 0.0)
    layout = jnp.where(column == DEAD_BUCKET, 0.0, sums[:2])
    return rel, layout[0], layout[1]


def ffn_kernel(
    unit, spots, core_ref, gain_ref, seed_ref, hidden_ref, gate_ref, up_ref, down_ref,
    out_ref, grad_ref, low_ref, dgain_ref, gate_away_ref, gate_stay_ref, up_away_ref,
    up_stay_ref, down_away_ref, down_stay_ref, out_sum, n_ref, turned_ref, ddown_ref,
):
    step = pl.program_id(0)
    slots, width = n_ref.shape
    half = width // 2
    rows = half // len(spots[0])

    def place(refs, spot, value):
        for ref, part in zip(refs, (value[:half], value[half:])):
            for at, to in enumerate(spot):
                ref[to * rows : (to + 1) * rows, :] = part[at * rows : (at + 1) * rows]

    @pl.when(step == 0)
    def _():
        for r in range(0, slots, 64):
            rows_now = hidden_ref[r : r + 64, :]
            out_sum[r : r + 64, :] = rows_now
            n_ref[r : r + 64, :] = norm_apply(rows_now, gain_ref[...]).astype(jnp.bfloat16)
        grad_ref[...] = jnp.zeros_like(grad_ref)
        core = core_ref[0]
        for lanes in range(0, width, 128):
            turned = n_ref[:, lanes : lanes + 128].T
            for part in range(128 // unit):
                group = lanes // unit + part
                first = jnp.where(core == group % 2, half, 0) + group // 2 * unit
                turned_ref[pl.ds(pl.multiple_of(first, 16), unit), :] = turned[
                    part * unit : (part + 1) * unit
                ]

    seed = seed_ref[...]
    w_gate, w_up, w_down = gate_ref[...], up_ref[...], down_ref[...]
    gate = plain_product(n_ref[...], w_gate)
    upper = plain_product(n_ref[...], w_up)
    grad_act = right_transposed(seed, w_down)
    square = gate * gate
    tanh = jnp.tanh(gelu_scale * (gate + 0.044715 * gate * square))
    cdf = 0.5 * (1.0 + tanh)
    gelu = gate * cdf
    slope = cdf + 0.5 * gate * (1.0 - tanh * tanh) * gelu_scale * (1.0 + 3 * 0.044715 * square)
    activated = (gelu * upper).astype(jnp.bfloat16)
    grad_gate = (grad_act * upper * slope).astype(jnp.bfloat16)
    grad_upper = (grad_act * gelu).astype(jnp.bfloat16)
    out_sum[...] += plain_product(activated, w_down)
    grad_ref[...] += right_transposed(
        jnp.concatenate([grad_gate, grad_upper], axis=1), jnp.concatenate([w_gate, w_up], axis=1)
    )
    d_gate = plain_product(turned_ref[...], grad_gate).astype(jnp.bfloat16)
    place((gate_away_ref, gate_stay_ref), spots[0], d_gate)
    d_up = plain_product(turned_ref[...], grad_upper).astype(jnp.bfloat16)
    place((up_away_ref, up_stay_ref), spots[1], d_up)
    tile = w_down.shape[0]
    ddown_ref[pl.ds(pl.multiple_of(step * tile, tile), tile), :] = left_transposed(
        activated, seed
    ).astype(jnp.bfloat16)

    @pl.when(step == pl.num_programs(0) - 1)
    def _():
        gain = gain_ref[...]
        gain_sum = jnp.zeros((1, width), jnp.float32)
        for r in range(0, slots, 64):
            here = slice(r, r + 64)
            out_ref[here, :] = out_sum[here, :].astype(jnp.bfloat16)
            value, grad = hidden_ref[here, :], grad_ref[here, :]
            scale = lax.rsqrt(jnp.mean(value * value, axis=1, keepdims=True) + epsilon)
            turn = value * scale
            gain_sum += jnp.sum(grad * turn, axis=0, keepdims=True)
            grad = grad * gain
            shift = jnp.mean(grad * turn, axis=1, keepdims=True)
            total = seed_ref[here, :].astype(jnp.float32) + scale * (grad - turn * shift)
            grad_ref[here, :] = total
            low_ref[here, :] = total.astype(jnp.bfloat16)
        dgain_ref[...] = gain_sum
        tall = ddown_ref.shape[0] // (2 * len(spots[2]))
        low_bits = unit // rows
        flip = core_ref[0] == 1
        for at, to in enumerate(spots[2]):
            first = (at // low_bits * 2 * low_bits + at % low_bits) * tall
            second = first + low_bits * tall
            zero = ddown_ref[first : first + tall, :]
            one = ddown_ref[second : second + tall, :]
            down_away_ref[to * tall : (to + 1) * tall, :] = jnp.where(flip, zero, one)
            down_stay_ref[to * tall : (to + 1) * tall, :] = jnp.where(flip, one, zero)


def ffn_call(core, unit, spots, gain, seed, hidden, packed, w_down):
    slots, width = hidden.shape
    ff = w_down.shape[0]
    tile = 256
    count = ff // tile
    single = pl.Buffered(1)
    full = pl.BlockSpec((slots, width), lambda f: (0, 0), pipeline_mode=single)
    column = pl.BlockSpec((width // 2, tile), lambda f: (0, f))
    row = pl.BlockSpec((tile, width), lambda f: (f, 0))
    down_half = pl.BlockSpec((ff // 2, width), lambda f: (0, 0), pipeline_mode=single)
    vector = pl.BlockSpec((1, width), lambda f: (0, 0))
    return pl.pallas_call(
        functools.partial(ffn_kernel, unit, spots),
        grid=(count,),
        in_specs=[
            pl.BlockSpec(memory_space=pltpu.SMEM),
            vector,
            full,
            full,
            pl.BlockSpec((width, tile), lambda f: (0, f)),
            pl.BlockSpec((width, tile), lambda f: (0, f + count)),
            row,
        ],
        out_specs=[full, full, full, vector] + [column] * 4 + [down_half] * 2,
        out_shape=[
            jax.ShapeDtypeStruct((slots, width), jnp.bfloat16),
            jax.ShapeDtypeStruct((slots, width), jnp.float32),
            jax.ShapeDtypeStruct((slots, width), jnp.bfloat16),
            jax.ShapeDtypeStruct((1, width), jnp.float32),
        ]
        + [jax.ShapeDtypeStruct((width // 2, ff), jnp.bfloat16)] * 4
        + [jax.ShapeDtypeStruct((ff // 2, width), jnp.bfloat16)] * 2,
        scratch_shapes=[
            pltpu.VMEM((slots, width), jnp.float32),
            pltpu.VMEM((slots, width), jnp.bfloat16),
            pltpu.VMEM((width, slots), jnp.bfloat16),
            pltpu.VMEM((ff, width), jnp.bfloat16),
        ],
        name="ffn",
        **params_for(18 * slots * width * ff, 50e6),
    )(core, gain, seed, hidden, packed, packed, w_down)


class Exchange:
    def __init__(self, mesh):
        self.count = mesh.shape["wide"] * mesh.shape["narrow"]
        self.bits = self.count.bit_length() - 1
        assert self.count == 1 << self.bits
        one, two, three, *tail = [b for b in range(self.bits) if b != CORE_BIT]
        self.orders = (
            [CORE_BIT, one, two] + tail + [three],
            [CORE_BIT, two, three, one] + tail,
            [CORE_BIT, three, one, two] + tail,
        )

    def me(self):
        return lax.axis_index(AXES)

    def mine(self, bit):
        return (self.me() >> bit) & 1

    def swap(self, value, bit):
        pairs = [(d, d ^ (1 << bit)) for d in range(self.count)]
        return lax.ppermute(value, AXES, pairs)

    def spots(self, order):
        held = [b for b in range(self.bits - 1, -1, -1) if b != CORE_BIT]
        steps = self.orders[order][1:]
        last = len(held) - 1
        found = []
        for at in range(1 << len(held)):
            value = {bit: at >> (last - k) & 1 for k, bit in enumerate(held)}
            found.append(sum(value[bit] << (last - k) for k, bit in enumerate(steps)))
        return tuple(found)

    def spread(self, shard):
        copies = jnp.broadcast_to(shard[None], (self.count,) + shard.shape)
        return lax.all_to_all(copies, AXES, 0, 0, tiled=True)

    def sum_small(self, terms):
        return jnp.sum(lax.all_to_all(terms, AXES, 0, 0, tiled=True), axis=0)


class Gather:
    def __init__(self, exchange, shard, order):
        self.exchange = exchange
        self.value = shard[None]
        self.steps = list(reversed(exchange.orders[order]))
        self.offsets = [0]
        self.flight = None

    def done(self):
        return not self.steps

    def go(self):
        self.flight = self.exchange.swap(self.value, self.steps[0])

    def land(self):
        bit = self.steps.pop(0)
        other, self.flight = self.flight, None
        self.offsets += [offset | 1 << bit for offset in self.offsets]
        if self.steps:
            self.value = jnp.concatenate([self.value, other], axis=0)
        else:
            self.other = other


def project_kernel(offsets, me_ref, x_ref, *refs):
    count = len(offsets)
    halves, outs, scratch = refs[: 2 * count], refs[2 * count : 4 * count], refs[4 * count]
    me = me_ref[0]
    for at in range(count):
        value_ref, other_ref = halves[2 * at : 2 * at + 2]
        out_ref, full_ref = outs[2 * at : 2 * at + 2]
        places, rows, _ = value_ref.shape
        for place, offset in enumerate(offsets[at]):
            part = value_ref[place] if place < places else other_ref[place - places]
            begin = pl.multiple_of((me ^ offset) * rows, rows)
            scratch[at, pl.ds(begin, rows), :] = part
        full_ref[...] = scratch[at]
        out_ref[...] = plain_product(x_ref[...], scratch[at]).astype(jnp.bfloat16)


def project_call(exchange, normed, tasks):
    places, rows, inner = tasks[0].value.shape
    slots, width = normed.shape
    if rows % 16:
        fulls, outs = [], []
        for task in tasks:
            held = jnp.concatenate([task.value, task.other], axis=0)
            place_of = np.argsort(np.asarray(task.offsets))
            spots = jnp.asarray(place_of)[exchange.me() ^ jnp.arange(exchange.count)]
            fulls.append(jnp.take(held, spots, axis=0).reshape(width, inner))
            outs.append(plain_product(normed, fulls[-1]).astype(jnp.bfloat16))
        return outs, fulls
    tile = 256
    part = pl.BlockSpec((places, rows, tile), lambda n: (0, 0, n))
    column = pl.BlockSpec((slots, tile), lambda n: (0, n))
    full = pl.BlockSpec((width, tile), lambda n: (0, n))
    results = pl.pallas_call(
        functools.partial(project_kernel, tuple(tuple(task.offsets) for task in tasks)),
        grid=(inner // tile,),
        in_specs=[
            pl.BlockSpec(memory_space=pltpu.SMEM),
            pl.BlockSpec((slots, width), lambda n: (0, 0)),
        ]
        + [part] * (2 * len(tasks)),
        out_specs=[column, full] * len(tasks),
        out_shape=[
            jax.ShapeDtypeStruct((slots, inner), jnp.bfloat16),
            jax.ShapeDtypeStruct((width, inner), jnp.bfloat16),
        ]
        * len(tasks),
        scratch_shapes=[pltpu.VMEM((len(tasks), width, tile), jnp.bfloat16)],
        name="project",
        **params_for(2 * len(tasks) * slots * width * inner, 20e6),
    )(
        exchange.me().astype(jnp.int32).reshape(1),
        normed,
        *[half for task in tasks for half in (task.value, task.other)],
    )
    return results[0::2], results[1::2]


class Scatter:
    def __init__(self, exchange, terms, order, away=None):
        self.exchange = exchange
        self.held = list(range(exchange.bits - 1, -1, -1))
        if away is not None:
            self.held = exchange.orders[order][1:]
        dims = (2,) * len(self.held)
        rows = terms.shape[0] >> len(self.held)
        self.value = terms.reshape(dims + (rows,) + terms.shape[1:])
        self.away = None if away is None else away.reshape(self.value.shape)
        self.steps = list(exchange.orders[order])
        self.flight = None

    def done(self):
        return not self.steps

    def go(self):
        bit = self.steps[0]
        if self.away is not None:
            self.flight = self.exchange.swap(self.away, bit)
            return
        self.spot = self.held.index(bit)
        away = lax.dynamic_index_in_dim(
            self.value, 1 - self.exchange.mine(bit), self.spot, keepdims=False
        )
        self.flight = self.exchange.swap(away, bit)

    def land(self):
        bit = self.steps.pop(0)
        other, self.flight = self.flight, None
        stay = self.value
        if self.away is None:
            stay = lax.dynamic_index_in_dim(
                self.value, self.exchange.mine(bit), self.spot, keepdims=False
            )
            self.held.pop(self.spot)
        self.away = None
        value = stay.astype(jnp.float32) + other.astype(jnp.float32)
        if self.steps:
            value = value.astype(jnp.bfloat16)
        self.value = value


class Traffic:
    limit = 5

    def __init__(self):
        self.tasks = []

    def add(self, *tasks):
        self.tasks += tasks
        self.send()

    def send(self):
        busy = sum(task.flight is not None for task in self.tasks)
        for task in self.tasks:
            if task.flight is None and busy < self.limit:
                task.go()
                busy += 1

    def step(self, *work):
        flying = [task for task in self.tasks if task.flight is not None]
        work, flights = lax.optimization_barrier((work, [task.flight for task in flying]))
        for task, flight in zip(flying, flights):
            task.flight = flight
            task.land()
        self.tasks = [task for task in self.tasks if not task.done()]
        self.send()
        return work[0] if len(work) == 1 else work


def norm_apply(values, gain):
    return values * lax.rsqrt(jnp.mean(values * values, axis=-1, keepdims=True) + epsilon) * gain


def layer(
    exchange, inputs, norm_first, w_query, w_key, w_value, w_out, rel_table, x_table, y_table,
    norm_second, w_gate, w_up, w_down, lengths, boxes, cotangent,
):
    seq_count, slots, width = inputs.shape
    inner = w_query.shape[1]
    count = exchange.count
    entries = rel_table.shape[0]
    span = norm_first.shape[0]

    rows = inputs.reshape(slots, width).astype(jnp.float32)
    seed = cotangent.reshape(slots, width)
    traffic = Traffic()
    qkv_tasks = [
        Gather(exchange, shard, order) for order, shard in enumerate((w_query, w_key, w_value))
    ]
    traffic.add(*qkv_tasks)
    longest = max(span, entries)
    small = exchange.spread(
        jnp.stack(
            [
                jnp.pad(part, (0, longest - part.shape[0]))
                for part in (norm_first, norm_second, rel_table, x_table, y_table)
            ]
        )
    ).reshape(count, 5, longest)
    packed = lax.all_gather(
        jnp.concatenate([w_gate, w_up, w_out], axis=1), AXES, axis=0, tiled=True
    )
    down_full = lax.all_gather(w_down, AXES, axis=0, tiled=True)
    ix, iy, ix_twice, iy_twice = index_call(lengths, traffic.step(boxes)[0])
    gain_one = small[:, 0, :span].reshape(-1).astype(jnp.float32)
    gain_two = small[:, 1, :span].reshape(-1).astype(jnp.float32)
    tables = jnp.concatenate(
        [small[:, 2 + at, :entries].reshape(HEADS, BUCKETS) for at in range(3)], axis=1
    )
    lhs, skew = prepare_call(tables, slots)
    blocks = slots // BIAS_TILE
    bias = None
    cuts = [0, blocks // 4, blocks // 4 * 3, blocks] + [blocks] * (exchange.bits - 5)
    for begin, end in zip(cuts[:-1], cuts[1:]):
        if bias is None:
            lhs = traffic.step(lhs)
        else:
            lhs, bias = traffic.step(lhs, bias)
        if end > begin:
            bias = bias_call(ix_twice, iy_twice, lhs, skew, begin, end, bias)
    normed_one = norm_apply(rows, gain_one).astype(jnp.bfloat16)
    normed_one, bias = traffic.step(normed_one, bias)
    projected, fulls = project_call(exchange, normed_one, qkv_tasks)
    query, key_rows, value_rows = projected
    query_full, key_full, value_full = fulls
    probs, mixed = attend_call(query, key_rows, value_rows, bias)
    out_full = packed[:, 2 * w_gate.shape[1] :]
    hidden = rows + plain_product(mixed, out_full)
    core = exchange.mine(CORE_BIT).astype(jnp.int32).reshape(1)
    unit = width // count << CORE_BIT
    spots = tuple(exchange.spots(order) for order in range(3))
    output, grad_hidden, branch_low, grad_gain_two, *halves = ffn_call(
        core, unit, spots, gain_two.reshape(1, -1), seed, hidden, packed, down_full
    )
    ffn_tasks = [
        Scatter(exchange, halves[2 * at + 1], at, halves[2 * at]) for at in range(3)
    ]
    traffic.add(*ffn_tasks)
    d_out = left_transposed(mixed, branch_low).astype(jnp.bfloat16)
    grad_mixed = right_transposed(branch_low, out_full).astype(jnp.bfloat16)
    grad_mixed, d_out = traffic.step(grad_mixed, d_out)
    pairs = inner // 128
    cuts = (0, pairs)
    back = None
    for begin, end in zip(cuts[:-1], cuts[1:]):
        back = attend_back_call(
            query, key_rows, value_rows, grad_mixed, probs, begin, end, back
        )
        back = traffic.step(back)
    ds, dq, dk, dv = back
    d_weights = [left_transposed(normed_one, part).astype(jnp.bfloat16) for part in (dq, dk, dv)]
    grad_normed_one = (
        right_transposed(dq, query_full)
        + right_transposed(dk, key_full)
        + right_transposed(dv, value_full)
    )
    grad_normed_one, d_weights = traffic.step(grad_normed_one, d_weights)
    half = width // 2
    d_weights[0] = jnp.concatenate([d_weights[0], d_out[:, :half]], axis=1)
    d_weights[1] = jnp.concatenate([d_weights[1], d_out[:, half:]], axis=1)
    w_tasks = [Scatter(exchange, part, at) for at, part in enumerate(d_weights)]
    traffic.add(*w_tasks)
    unused_one, norm_one_pull = jax.vjp(norm_apply, rows, gain_one)
    rows_part, grad_gain_one = norm_one_pull(grad_normed_one)
    grad_inputs = (grad_hidden + rows_part).reshape(inputs.shape)
    parts = []
    pieces = 3
    for piece in range(pieces):
        begin, end = piece * blocks // pieces, (piece + 1) * blocks // pieces
        parts.append(table_call(ds, ix, iy, begin, end))
        ix, parts = traffic.step(ix, parts)
    grad_rel, grad_x, grad_y = table_finish(parts)
    g_small = exchange.sum_small(
        jnp.concatenate(
            [
                part.reshape(count, -1)
                for part in (grad_gain_one, grad_gain_two, grad_rel, grad_x, grad_y)
            ],
            axis=1,
        )
    )
    while traffic.tasks:
        g_small = traffic.step(g_small)
    g_gate, g_up, g_down = (task.value for task in ffn_tasks)
    edges = [0, span, 2 * span, 2 * span + entries, 2 * span + 2 * entries, g_small.shape[0]]
    g_small = [g_small[a:b] for a, b in zip(edges[:-1], edges[1:])]
    return (
        output.reshape(inputs.shape),
        grad_inputs,
        g_small[0],
        w_tasks[0].value[:, :inner],
        w_tasks[1].value[:, :inner],
        w_tasks[2].value,
        jnp.concatenate([task.value[:, inner:] for task in w_tasks[:2]], axis=1),
        g_small[2],
        g_small[3],
        g_small[4],
        g_small[1],
        g_gate,
        g_up,
        g_down,
    )


def solution(mesh):
    exchange = Exchange(mesh)
    vector, matrix, cube = P(AXES), P(AXES, None), P(AXES, None, None)
    in_specs = (
        (cube, vector)
        + (matrix,) * 4
        + (vector,) * 4
        + (matrix,) * 3
        + (vector, cube, cube)
    )
    out_specs = (cube, cube, vector) + (matrix,) * 4 + (vector,) * 4 + (matrix,) * 3

    def local(*args):
        return layer(exchange, *args)

    return jax.shard_map(local, mesh=mesh, in_specs=in_specs, out_specs=out_specs, check_vma=False)
```
